512 devices in a mesh: space: 64 (over y, z), dp: 8 (over x, core).
Axes of the slice: x: 4, y: 4, z: 16, core: 2. Of those that a mesh axis runs over, the one named last changes fastest.
Arguments:
- coarse_latents: bfloat16 [8, 4096, 512], P('dp', 'space'), may hold values from -6 to 6
- active_blocks: int32 [8, 128], P('dp'), may hold values from 0 to 4095, as said below
- face_links: int32 [8, 128, 6], P('dp', 'space'), may hold values from -1 to 127, as said below
- cotangent: bfloat16 [8, 128, 8, 8, 256], P('dp', 'space'), may hold values from -6 to 6
- up_weight: bfloat16 [64, 2048], replicated, may hold values from -0.75 to 0.75
- conv_one: bfloat16 [27, 32, 32], replicated, may hold values from -0.21875 to 0.21875
- conv_two: bfloat16 [27, 32, 32], replicated, may hold values from -0.21875 to 0.21875
Outputs:
- fine: bfloat16 [8, 128, 8, 8, 256], P('dp', 'space')
- grad_one: float32 [27, 32, 32], replicated
- grad_two: float32 [27, 32, 32], replicated
The draws below stay inside these ranges and needn't reach their ends.
Inputs may be any that keep to these rules, and one draw needn't show every extreme that they name: `active_blocks`: call the bricks at positions i * 2 to (i + 1) * 2 - 1 group i and the block rows i * 64 to (i + 1) * 64 - 1 range i. At most 2 bricks of one group take their blocks from one range, and in every scene every group has exactly 2 from some range. `face_links`: links are mutual: if brick h is the neighbour of g across face f, g is the neighbour of h across the opposite face. A neighbour of brick g lies at a position whose quotient by 2 differs from that of g by at most one; across a -x, -y or -z face that quotient is never larger than that of g, across a +x, +y or +z face never smaller.
All inputs are finite; a program needn't handle non-finite values.
Results may differ from the reference program's by a relative error of at most 0.0057.
Values may be sent and summed in bfloat16 or wider, within the bound.
A program may use at most 128 MiB of HBM per device.

```python
import math
import jax
import jax.numpy as jnp
from jax import lax

C = 64
F = 32
EDGE = 8
PEER_MOST = 2
BR_DEV = 2
BLK_DEV = 64
SCENES = 8
BRICKS = 128
BLOCKS = 4096


def row_permutations(seed_key, row_count, length):
    subkeys = jax.random.split(seed_key, row_count)
    return jax.vmap(lambda subkey: jax.random.permutation(subkey, length))(subkeys).astype(jnp.int32)


def draw_active_blocks(key, part):
    devices = BRICKS // BR_DEV

    def scene_active(scene_key):
        key_perm, key_start, key_forced, key_other, key_local = jax.random.split(scene_key, 5)
        offsets_perm = row_permutations(key_perm, devices, devices)
        start = jax.random.randint(key_start, (devices,), 0, devices).astype(jnp.int32)
        forced = jax.random.randint(key_forced, (), 0, devices).astype(jnp.int32)
        other = (forced + 1 + jax.random.randint(key_other, (), 0, devices - 1)) % devices
        device_index = jnp.arange(devices, dtype=jnp.int32)
        start = jnp.where(device_index == forced, devices // 2, start)
        start = jnp.where(device_index == other, devices - 1, start)
        rotated = (offsets_perm - offsets_perm[:, :1] + start[:, None]) % devices
        column = jnp.maximum(jnp.arange(BR_DEV, dtype=jnp.int32) - PEER_MOST + 1, 0)
        offsets = rotated[:, column]
        owners = (device_index[:, None] + offsets) % devices
        local = jax.random.randint(key_local, (devices, BR_DEV), 0, BLK_DEV).astype(jnp.int32)
        return (owners * BLK_DEV + local).reshape(-1).astype(jnp.int32)
    return jax.vmap(scene_active)(jax.random.split(key, SCENES))


def draw_face_links(key, part):
    devices = BRICKS // BR_DEV

    def scene_links(scene_key):
        columns = []
        for axis_index in range(3):
            key_perm, key_shift, key_keep = jax.random.split(jax.random.fold_in(scene_key, axis_index + 11), 3)
            local_perm = row_permutations(key_perm, devices, BR_DEV)
            bases = jnp.arange(devices, dtype=jnp.int32)[:, None] * BR_DEV
            ordering = (bases + local_perm).reshape(-1)
            inverse = (bases + jnp.argsort(local_perm, axis=1).astype(jnp.int32)).reshape(-1)
            stride = jax.random.randint(key_shift, (), 1, BR_DEV + 1)
            keeping = jax.random.randint(key_keep, (BRICKS,), 0, 4) > 0
            upper = inverse + stride
            upper_safe = jnp.minimum(upper, BRICKS - 1)
            plus = jnp.where((upper < BRICKS) & keeping[inverse], ordering[upper_safe], -1)
            lower = inverse - stride
            lower_safe = jnp.maximum(lower, 0)
            minus = jnp.where((lower >= 0) & keeping[lower_safe], ordering[lower_safe], -1)
            columns.append(minus)
            columns.append(plus)
        return jnp.stack(columns, axis=1).astype(jnp.int32)
    return jax.vmap(scene_links)(jax.random.split(key, SCENES))


def levels(stream_key, dims, shards, smallest, top_value):
    def one(dim, blocks):
        heights = jax.random.uniform(jax.random.fold_in(jax.random.fold_in(stream_key, 6), dim), (blocks,), jnp.float32, smallest / len(shards), top_value / len(shards))
        return jnp.repeat(jnp.exp(heights), dims[dim] // blocks).reshape((-1,) + (1,) * (len(dims) - dim - 1))

    loudness = one(*shards[0])
    for cut in shards[1:]:
        loudness = loudness * one(*cut)
    return loudness


def bell_draw(key, extent, spread, most, cuts=(), kind=jnp.bfloat16):
    drawn = jax.random.normal(key, extent, jnp.float32) * spread
    if len(cuts) > 0:
        drawn = levels(key, extent, cuts, -0.22, 0.18) * drawn
    return jnp.clip(drawn, min=-most, max=most).astype(kind)


def setup_inputs(seed: int = 0) -> dict:
    splits = jax.random.split(jax.random.key(seed), 8)
    return {
        "coarse_latents": bell_draw(splits[0], (SCENES, BLOCKS, 8 * C), 1.0, 6.0, ((0, 8), (1, 64))),
        "active_blocks": draw_active_blocks(jax.random.fold_in(splits[7], 71), 0),
        "face_links": draw_face_links(jax.random.fold_in(splits[7], 71), 0),
        "cotangent": bell_draw(splits[3], (SCENES, BRICKS, EDGE, EDGE, EDGE * F), 1.0, 6.0, ((0, 8), (1, 64))),
        "up_weight": bell_draw(splits[4], (C, (EDGE // 2) ** 3 * F), C ** -0.5, 0.75),
        "conv_one": bell_draw(splits[5], (27, F, F), (27 * F) ** -0.5, 0.21875),
        "conv_two": bell_draw(splits[6], (27, F, F), (27 * F) ** -0.5, 0.21875),
    }


def lift_bricks(latent_rows, up_weight):
    bricks_total = latent_rows.shape[0]
    blocks = latent_rows.reshape(bricks_total, 8, C).astype(jnp.float32)
    cells = jnp.einsum('nci,io->nco', blocks, up_weight.astype(jnp.float32))
    half = EDGE // 2
    shaped = cells.reshape(bricks_total, 2, 2, 2, half, half, half, F)
    shaped = shaped.transpose(0, 1, 4, 2, 5, 3, 6, 7)
    return shaped.reshape(bricks_total, EDGE, EDGE, EDGE, F).astype(jnp.bfloat16)

def pad_faces(volume, face_links):
    bricks_total = volume.shape[0]
    neighbour = jnp.maximum(face_links, 0)
    present = (face_links >= 0).astype(jnp.float32)[:, :, None, None, None]
    last = EDGE - 1
    padded = jnp.zeros((bricks_total, EDGE + 2, EDGE + 2, EDGE + 2, F), jnp.float32)
    padded = padded.at[:, 1:EDGE + 1, 1:EDGE + 1, 1:EDGE + 1].set(volume)
    padded = padded.at[:, 0, 1:EDGE + 1, 1:EDGE + 1].set(volume[neighbour[:, 0], last] * present[:, 0])
    padded = padded.at[:, EDGE + 1, 1:EDGE + 1, 1:EDGE + 1].set(volume[neighbour[:, 1], 0] * present[:, 1])
    padded = padded.at[:, 1:EDGE + 1, 0, 1:EDGE + 1].set(volume[neighbour[:, 2], :, last] * present[:, 2])
    padded = padded.at[:, 1:EDGE + 1, EDGE + 1, 1:EDGE + 1].set(volume[neighbour[:, 3], :, 0] * present[:, 3])
    padded = padded.at[:, 1:EDGE + 1, 1:EDGE + 1, 0].set(volume[neighbour[:, 4], :, :, last] * present[:, 4])
    padded = padded.at[:, 1:EDGE + 1, 1:EDGE + 1, EDGE + 1].set(volume[neighbour[:, 5], :, :, 0] * present[:, 5])
    return padded

def window_at(padded, start_x, start_y, start_z):
    return padded[:, start_x:start_x + EDGE, start_y:start_y + EDGE, start_z:start_z + EDGE]

def conv_forward(padded, weights):
    total = jnp.zeros(padded.shape[:1] + (EDGE, EDGE, EDGE, F), jnp.float32)
    for offset_index in range(27):
        shift_x, shift_y, shift_z = (offset_index // 9, offset_index // 3 % 3, offset_index % 3)
        window = window_at(padded, shift_x, shift_y, shift_z)
        total = total + jnp.einsum('nxyzi,io->nxyzo', window, weights[offset_index])
    return total

def conv_backward(padded, weights):
    total = jnp.zeros(padded.shape[:1] + (EDGE, EDGE, EDGE, F), jnp.float32)
    for offset_index in range(27):
        shift_x, shift_y, shift_z = (offset_index // 9, offset_index // 3 % 3, offset_index % 3)
        window = window_at(padded, 2 - shift_x, 2 - shift_y, 2 - shift_z)
        total = total + jnp.einsum('nxyzo,io->nxyzi', window, weights[offset_index])
    return total

def weight_grad(padded, gradient):
    pieces = []
    for offset_index in range(27):
        shift_x, shift_y, shift_z = (offset_index // 9, offset_index // 3 % 3, offset_index % 3)
        window = window_at(padded, shift_x, shift_y, shift_z)
        pieces.append(jnp.einsum('nxyzi,nxyzo->io', window, gradient))
    return jnp.stack(pieces)

def reference(coarse_latents, active_blocks, face_links, cotangent, up_weight, conv_one, conv_two):
    weights_one = conv_one.astype(jnp.float32)
    weights_two = conv_two.astype(jnp.float32)

    def scene_step(inputs):
        coarse_scene, active_scene, links_scene, upstream = inputs
        lifted = lift_bricks(coarse_scene[active_scene], up_weight).astype(jnp.float32)
        lifted_pad = pad_faces(lifted, links_scene)
        pre = conv_forward(lifted_pad, weights_one)
        hidden = jax.nn.silu(pre).astype(jnp.bfloat16).astype(jnp.float32)
        hidden_pad = pad_faces(hidden, links_scene)
        fine = (lifted + conv_forward(hidden_pad, weights_two)).astype(jnp.bfloat16)
        upstream_full = upstream.reshape(BRICKS, EDGE, EDGE, EDGE, F).astype(jnp.float32)
        back = conv_backward(pad_faces(upstream_full, links_scene), weights_two)
        sigmoid = jax.nn.sigmoid(pre)
        grad_pre = (back * sigmoid * (1.0 + pre * (1.0 - sigmoid))).astype(jnp.bfloat16).astype(jnp.float32)
        second = weight_grad(hidden_pad, upstream_full)
        first = weight_grad(lifted_pad, grad_pre)
        return (fine.reshape(BRICKS, EDGE, EDGE, EDGE * F), first, second)
    fine, firsts, seconds = lax.map(scene_step, (coarse_latents, active_blocks, face_links, cotangent))
    scale = 1.0 / math.sqrt(SCENES * BRICKS * EDGE ** 3)
    return (fine, lax.optimization_barrier(jnp.sum(firsts, axis=0)) * scale, lax.optimization_barrier(jnp.sum(seconds, axis=0)) * scale)
```

```python
import math

import jax
import jax.numpy as jnp
from jax import lax
from jax.experimental import pallas as pl
from jax.experimental.pallas import tpu as pltpu
from jax.sharding import PartitionSpec as P


def passed_along(value, axis, steps):
    count = lax.axis_size(axis)
    first, last = (max(0, -steps), min(count, count - steps))
    return lax.ppermute(value, axis, [(source, source + steps) for source in range(first, last)])


def depth_select(extent):
    inputs_z = jnp.arange(extent + 2)[None, :, None]
    outputs_z = jnp.arange(extent)[None, None, :]
    offsets_z = jnp.arange(3)[:, None, None]
    return (inputs_z == outputs_z + offsets_z).astype(jnp.float32)


def band_matrix(weights, extent):
    channels = weights.shape[1]
    cube = weights.astype(jnp.float32).reshape(3, 3, 3, channels, channels)
    banded = jnp.einsum(
        "dpq,abdio->abpiqo", depth_select(extent), cube, precision=lax.Precision.HIGHEST
    )
    return banded.reshape(3, 3, (extent + 2) * channels, extent * channels).astype(jnp.bfloat16)


def apply_band(padded, banded, extent):
    total = None
    for shift_x in range(3):
        for shift_y in range(3):
            window = padded[:, shift_x : shift_x + extent, shift_y : shift_y + extent, :]
            term = jnp.einsum(
                "nxyp,pq->nxyq",
                window,
                banded[shift_x, shift_y],
                preferred_element_type=jnp.float32,
            )
            total = term if total is None else total + term
    return total


def band_gradient(padded, gradient, extent, channels):
    select = depth_select(extent)
    pieces = []
    for shift_x in range(3):
        for shift_y in range(3):
            window = padded[:, shift_x : shift_x + extent, shift_y : shift_y + extent, :]
            outer = jnp.einsum(
                "nxyp,nxyq->pq", window, gradient, preferred_element_type=jnp.float32
            )
            outer = outer.reshape(extent + 2, channels, extent, channels)
            pieces.append(
                jnp.einsum("dpq,piqo->dio", select, outer, precision=lax.Precision.HIGHEST)
            )
    return jnp.stack(pieces).reshape(27, channels, channels)


def lift_bricks(latent_rows, up_weight, extent, channels):
    bricks_here = latent_rows.shape[0]
    blocks = latent_rows.reshape(bricks_here, 8, -1)
    cells = jnp.einsum("nci,io->nco", blocks, up_weight, preferred_element_type=jnp.float32)
    half = extent // 2
    shaped = cells.reshape(bricks_here, 2, 2, 2, half, half, half, channels)
    shaped = shaped.transpose(0, 1, 4, 2, 5, 3, 6, 7)
    return shaped.reshape(bricks_here, extent, extent, extent * channels).astype(jnp.bfloat16)


def face_planes(volume, channels):
    bricks_here, extent = (volume.shape[0], volume.shape[1])
    planes = [
        volume[:, 0],
        volume[:, extent - 1],
        volume[:, :, 0],
        volume[:, :, extent - 1],
        volume[:, :, :, 0:channels],
        volume[:, :, :, (extent - 1) * channels :],
    ]
    return jnp.stack([one_plane.reshape(bricks_here, -1) for one_plane in planes], axis=1)


def share_faces(stacked):
    from_left = passed_along(stacked, "space", 1)
    from_right = passed_along(stacked, "space", -1)
    return jnp.stack([from_left, stacked, from_right], axis=1)


def fill_padding(volume, face_pool, face_links, position, channels):
    bricks_here, extent = (volume.shape[0], volume.shape[1])
    neighbour = jnp.maximum(face_links, 0)
    source = jnp.clip(neighbour // bricks_here - position + 1, 0, 2)
    face_index = jnp.arange(6, dtype=jnp.int32)[None, :]
    row_index = (source * bricks_here + neighbour % bricks_here) * 6 + (face_index ^ 1)
    flattened = face_pool.reshape(3 * bricks_here * 6, -1)
    picked = jnp.take(flattened, row_index.reshape(-1), axis=0).reshape(bricks_here, 6, -1)
    picked = jnp.where((face_links >= 0)[:, :, None], picked, jnp.zeros((), picked.dtype))
    padded = jnp.pad(volume, ((0, 0), (1, 1), (1, 1), (channels, channels)))
    inside_range = slice(1, extent + 1)
    middle_range = slice(channels, (extent + 1) * channels)
    flat_face = (bricks_here, extent, extent * channels)
    depth_face = (bricks_here, extent, extent, channels)
    padded = padded.at[:, 0, inside_range, middle_range].set(picked[:, 0].reshape(flat_face))
    padded = padded.at[:, extent + 1, inside_range, middle_range].set(
        picked[:, 1].reshape(flat_face)
    )
    padded = padded.at[:, inside_range, 0, middle_range].set(picked[:, 2].reshape(flat_face))
    padded = padded.at[:, inside_range, extent + 1, middle_range].set(
        picked[:, 3].reshape(flat_face)
    )
    padded = padded.at[:, inside_range, inside_range, 0:channels].set(
        picked[:, 4].reshape(depth_face)
    )
    padded = padded.at[:, inside_range, inside_range, (extent + 1) * channels :].set(
        picked[:, 5].reshape(depth_face)
    )
    return padded


MESH_ID = pl.DeviceIdType.MESH


def sum_kernel(parts_ref, out_ref, first_buf, low_buf, high_buf, send_sems, recv_sems):
    space = lax.axis_index("space")
    dp = lax.axis_index("dp")
    row, depth = space // 16, space % 16
    low, high = depth % 4, depth // 4
    me = row * 8 + dp

    def wide(step):
        other = (me + step) % 32
        return other, {"space": (other // 8) * 16 + depth, "dp": other % 8}

    def near(step):
        return {"space": row * 16 + high * 4 + (low + step) % 4, "dp": dp}

    def far(step):
        return {"space": row * 16 + ((high + step) % 4) * 4 + low, "dp": dp}

    barrier = pltpu.get_barrier_semaphore()
    for step in range(1, 32):
        pl.semaphore_signal(barrier, inc=1, device_id=wide(step)[1], device_id_type=MESH_ID)
    for step in range(1, 4):
        pl.semaphore_signal(barrier, inc=1, device_id=near(step), device_id_type=MESH_ID)
        pl.semaphore_signal(barrier, inc=1, device_id=far(step), device_id_type=MESH_ID)
    pl.semaphore_wait(barrier, 37)

    def send(source, target, device, phase):
        pltpu.make_async_remote_copy(
            src_ref=source,
            dst_ref=target,
            send_sem=send_sems.at[phase],
            recv_sem=recv_sems.at[phase],
            device_id=device,
            device_id_type=MESH_ID,
        ).start()

    def finish(buffer, count, phase):
        part = buffer.at[pl.ds(0, count)]
        pltpu.make_async_copy(part, part, recv_sems.at[phase]).wait()

    def sent(buffer, count, phase):
        part = buffer.at[pl.ds(0, count)]
        pltpu.make_async_copy(part, part, send_sems.at[phase]).wait()

    for step in range(1, 32):
        other, device = wide(step)
        send(parts_ref.at[other], first_buf.at[me], device, 0)
    first_buf[me] = parts_ref[me]
    finish(first_buf, 31, 0)
    low_buf[low] = jnp.sum(first_buf[...], axis=0)
    for step in range(1, 4):
        send(low_buf.at[low], low_buf.at[low], near(step), 1)
    finish(low_buf, 3, 1)
    high_buf[high] = (low_buf[0] + low_buf[1]) + (low_buf[2] + low_buf[3])
    for step in range(1, 4):
        send(high_buf.at[high], high_buf.at[high], far(step), 2)
    finish(high_buf, 3, 2)
    out_ref[me] = (high_buf[0] + high_buf[1]) + (high_buf[2] + high_buf[3])
    for step in range(1, 32):
        send(out_ref.at[me], out_ref.at[me], wide(step)[1], 3)
    finish(out_ref, 31, 3)
    sent(first_buf, 31, 0)
    sent(low_buf, 3, 1)
    sent(high_buf, 3, 2)
    sent(out_ref, 31, 3)


def sum_everywhere(first, second):
    flat = jnp.concatenate([first.reshape(-1, 128), second.reshape(-1, 128)], axis=0)
    rows = flat.shape[0]
    parts = jnp.pad(flat, ((0, 512 - rows), (0, 0))).reshape(32, 16, 128)
    total = pl.pallas_call(
        sum_kernel,
        out_shape=jax.ShapeDtypeStruct((32, 16, 128), jnp.float32),
        in_specs=[pl.BlockSpec(memory_space=pltpu.VMEM)],
        out_specs=pl.BlockSpec(memory_space=pltpu.VMEM),
        scratch_shapes=[
            pltpu.VMEM((32, 16, 128), jnp.float32),
            pltpu.VMEM((4, 16, 128), jnp.float32),
            pltpu.VMEM((4, 16, 128), jnp.float32),
            pltpu.SemaphoreType.DMA((4,)),
            pltpu.SemaphoreType.DMA((4,)),
        ],
        compiler_params=pltpu.CompilerParams(collective_id=0, has_side_effects=True),
    )(parts)
    total = total.reshape(512, 128)
    half = rows // 2
    return total[:half].reshape(first.shape), total[half:rows].reshape(second.shape)


def body(coarse_latents, active_blocks, face_links, cotangent, up_weight, conv_one, conv_two):
    position = lax.axis_index("space")
    devices = lax.axis_size("space")
    bricks_here = face_links.shape[1]
    extent = cotangent.shape[2]
    channels = conv_one.shape[1]
    blocks_here = coarse_latents.shape[1]
    local_rows = coarse_latents[0]
    listed = active_blocks[0]
    mine = lax.dynamic_slice_in_dim(listed, position * bricks_here, bricks_here)
    owners = mine // blocks_here
    wanted = listed.reshape(devices, bricks_here)
    held = wanted // blocks_here == position
    local_index = jnp.clip(wanted - position * blocks_here, 0, blocks_here - 1)
    packed = jnp.where(
        held[:, :, None], jnp.take(local_rows, local_index, axis=0), jnp.zeros((), local_rows.dtype)
    )
    received = lax.all_to_all(packed, "space", split_axis=0, concat_axis=0, tiled=True)
    latent_rows = received[owners, jnp.arange(bricks_here)]
    lifted = lift_bricks(latent_rows, up_weight, extent, channels)
    links = face_links[0]
    upstream = cotangent[0]
    lifted_pool = share_faces(face_planes(lifted, channels)[None])[0]
    lifted_pad = fill_padding(lifted, lifted_pool, links, position, channels)
    band_one = band_matrix(conv_one, extent)
    band_two = band_matrix(conv_two, extent)
    band_back = band_matrix(jnp.flip(conv_two, axis=0).transpose(0, 2, 1), extent)
    pre = apply_band(lifted_pad, band_one, extent)
    hidden = jax.nn.silu(pre).astype(jnp.bfloat16)
    hidden_pool = share_faces(face_planes(hidden, channels)[None])[0]
    hidden_pad = fill_padding(hidden, hidden_pool, links, position, channels)
    fine = (lifted.astype(jnp.float32) + apply_band(hidden_pad, band_two, extent)).astype(
        jnp.bfloat16
    )
    scale = 1.0 / math.sqrt(lax.axis_size("dp") * devices * bricks_here * extent**3)
    second_local = band_gradient(hidden_pad, upstream, extent, channels) * scale
    upstream_pool = share_faces(face_planes(upstream, channels)[None])[0]
    upstream_pad = fill_padding(upstream, upstream_pool, links, position, channels)
    back = apply_band(upstream_pad, band_back, extent)
    sigmoid = jax.nn.sigmoid(pre)
    grad_pre = (back * sigmoid * (1.0 + pre * (1.0 - sigmoid))).astype(jnp.bfloat16)
    first_local = band_gradient(lifted_pad, grad_pre, extent, channels) * scale
    grad_one, grad_two = sum_everywhere(first_local, second_local)
    return (fine[None], grad_one, grad_two)


def solution(mesh):
    return jax.shard_map(
        body,
        mesh=mesh,
        in_specs=(
            P("dp", "space", None),
            P("dp", None),
            P("dp", "space", None),
            P("dp", "space", None, None, None),
            P(),
            P(),
            P(),
        ),
        out_specs=(P("dp", "space", None, None, None), P(), P()),
        check_vma=False,
    )
```

```python
import math

import jax
import jax.numpy as jnp
from jax import lax
from jax.experimental import pallas as pl
from jax.experimental.pallas import tpu as pltpu
from jax.sharding import PartitionSpec as P

MESH_ID = pl.DeviceIdType.MESH
F32 = jnp.float32
BF16 = jnp.bfloat16


def iota(shape, dim):
    return lax.broadcasted_iota(jnp.int32, shape, dim)


def picked_rows(active_ref, coarse_ref, position):
    rows = 528
    group = ((iota((rows, 128), 0) >> 2) + 126) & 127
    listed = active_ref[...].astype(F32)
    mine = jnp.where(group == iota((rows, 128), 1), listed, 0.0)
    column = jnp.sum(mine, axis=1, keepdims=True)
    local = column - (position * 64).astype(F32)
    quarter = ((iota((rows, 256), 0) & 3) * 64).astype(F32)
    held = (local >= 0.0) & (local < 64.0)
    target = jnp.where(held, local, -1000.0) + quarter
    chosen = jnp.where(iota((rows, 256), 1).astype(F32) == target, 1.0, 0.0).astype(BF16)
    source = jnp.concatenate([coarse_ref[:, k * 128 : (k + 1) * 128] for k in range(4)], axis=0)
    return jnp.dot(chosen, source, preferred_element_type=F32)


def repeat_weights(weight_ref):
    pattern = jnp.where((iota((32, 256), 1) & 31) == iota((32, 256), 0), 1.0, 0.0).astype(BF16)
    return jnp.dot(weight_ref[...], pattern, preferred_element_type=F32)


def fill_band(band_ref, rep_ref):
    block = iota((32, 256), 1) >> 5
    for a in range(3):
        for b in range(3):
            base = (a * 3 + b) * 96
            low = rep_ref[base : base + 32, :]
            mid = rep_ref[base + 32 : base + 64, :]
            high = rep_ref[base + 64 : base + 96, :]
            for zi in range(8):
                strip = jnp.where(block == zi - 1, high, 0.0)
                strip = jnp.where(block == zi, mid, strip)
                strip = jnp.where(block == zi + 1, low, strip)
                first = b * 256 + zi * 32
                band_ref[a, first : first + 32, :] = strip.astype(BF16)
            first = 768 + b * 64
            band_ref[a, first : first + 32, :] = jnp.where(block == 0, low, 0.0).astype(BF16)
            band_ref[a, first + 32 : first + 64, :] = jnp.where(block == 7, high, 0.0).astype(BF16)
        band_ref[a, 960:1024, :] = jnp.zeros((64, 256), BF16)


def fill_band_back(band_ref, rep_ref):
    block = iota((32, 256), 1) >> 5
    for a in range(3):
        faces_first = jnp.zeros((32, 256), F32)
        faces_last = jnp.zeros((32, 256), F32)
        for b in range(3):
            base = ((2 - a) * 3 + 2 - b) * 96
            low = rep_ref[base : base + 32, :]
            mid = rep_ref[base + 32 : base + 64, :]
            high = rep_ref[base + 64 : base + 96, :]
            for zo in range(8):
                strip = jnp.where(block == zo + 1, low, 0.0)
                strip = jnp.where(block == zo, mid, strip)
                strip = jnp.where(block == zo - 1, high, strip)
                band_ref[a, zo * 32 : zo * 32 + 32, b * 256 : b * 256 + 256] = strip.astype(BF16)
            faces_first = jnp.where(block == 2 * b, high, faces_first)
            faces_last = jnp.where(block == 2 * b + 1, low, faces_last)
        band_ref[a, 0:32, 768:1024] = faces_first.astype(BF16)
        band_ref[a, 32:224, 768:1024] = jnp.zeros((192, 256), BF16)
        band_ref[a, 224:256, 768:1024] = faces_last.astype(BF16)


def fill_lift(lift_ref, up_ref):
    lift_ref[...] = jnp.zeros((512, 1024), BF16)
    for ky in range(4):
        for kx in range(4):
            part = up_ref[:, (kx * 4 + ky) * 128 : (kx * 4 + ky + 1) * 128]
            for c in range(2):
                row = ky * 128 + c * 64
                lane = kx * 256 + c * 128
                lift_ref[row : row + 64, lane : lane + 128] = part


def chosen_neighbour(links_ref, position, brick, face, before, own, after):
    link = links_ref[brick, face]
    if face % 2 == 0:
        outer, first = before, jnp.where(position > 0, 2 * position - 2, -8)
    else:
        outer, first = after, 2 * position + 2
    total = None
    for slices, base in ((outer, first), (own, 2 * position)):
        for m in range(2):
            mask = jnp.where(link == base + m, 1.0, 0.0).astype(F32)
            term = slices[m] * mask
            total = term if total is None else total + term
    return total


def fill_windows(win_ref, links_ref, position, before, own, after):
    row = iota((8, 8, 256), 1)
    row_face = iota((8, 256), 0)
    lane = iota((8, 8, 128), 2)
    row_half = iota((8, 8, 128), 1)
    shifted = []
    faces = []
    for n in range(2):
        volume = own(n)

        def neighbour(face, part):
            sources = [[part(f, m) for m in range(2)] for f in (before, own, after)]
            return chosen_neighbour(links_ref, position, n, face, *sources)

        y_minus = neighbour(2, lambda f, m: f(m)[:, 7:8, :])
        y_plus = neighbour(3, lambda f, m: f(m)[:, 0:1, :])
        back_one = jnp.where(row == 0, y_minus, pltpu.roll(volume, 1, 1))
        ahead_one = jnp.where(row == 7, y_plus, pltpu.roll(volume, 7, 1))
        z_minus = neighbour(4, lambda f, m: f(m)[:, :, 128:256])
        z_plus = neighbour(5, lambda f, m: f(m)[:, :, 0:128])
        pair = pltpu.roll(jnp.where(lane >= 64, z_minus, z_plus), 32, 2)
        pair = jnp.where(lane < 64, pair, 0.0)
        first = jnp.where(row_half == 0, 0.0, pltpu.roll(pair, 1, 1)) + pltpu.roll(pair, 64, 2)
        second = jnp.where(row_half == 7, 0.0, pltpu.roll(pair, 7, 1))
        shifted.append((back_one, volume, ahead_one, first, second))
        ends = []
        for face, x in ((0, 7), (1, 0)):
            plane = neighbour(face, lambda f, m: f(m)[x])
            ends.append(
                (
                    jnp.where(row_face == 0, 0.0, pltpu.roll(plane, 1, 0)),
                    plane,
                    jnp.where(row_face == 7, 0.0, pltpu.roll(plane, 7, 0)),
                )
            )
        faces.append(ends)
    for k in range(5):
        both = jnp.concatenate([shifted[0][k], shifted[1][k]], axis=1).astype(BF16)
        first = k * 256 if k < 4 else 896
        win_ref[1:9, :, first : first + both.shape[2]] = both
    for end, x in ((0, 0), (1, 9)):
        for k in range(3):
            both = jnp.concatenate([faces[0][end][k], faces[1][end][k]], axis=0)
            win_ref[x, :, k * 256 : k * 256 + 256] = both.astype(BF16)
        win_ref[x, :, 768:1024] = jnp.zeros((16, 256), BF16)


def window(win_ref, a):
    return win_ref[a : a + 8].reshape(128, 1024)


def convolve(win_ref, band_ref):
    total = None
    for a in range(3):
        term = jnp.dot(window(win_ref, a), band_ref[a], preferred_element_type=F32)
        total = term if total is None else total + term
    return total


def convolve_back(win_ref, band_ref):
    total = None
    for a in range(3):
        term = lax.dot_general(
            window(win_ref, a), band_ref[a], (((1,), (1,)), ((), ())), preferred_element_type=F32
        )
        total = term if total is None else total + term
    return total


def weight_products(turned, win_ref, parts_ref, first_part, reverse):
    block = iota((32, 256), 1) >> 5
    block_half = iota((32, 128), 1) >> 5
    sums = [None] * 28
    sums[27] = jnp.zeros((32, 128), F32)
    for a in range(3):
        seen = window(win_ref, a)
        faces = jnp.dot(turned, seen[:, 768:1024], preferred_element_type=F32)
        for b in range(3):
            outer = jnp.dot(turned, seen[:, b * 256 : b * 256 + 256], preferred_element_type=F32)
            half = (b // 2) * 128
            for dz in range(3):
                total = None
                for z in range(8):
                    zi = z + dz - 1
                    if 0 <= zi < 8:
                        side = slice(0, 128) if zi < 4 else slice(128, 256)
                        strip = outer[z * 32 : z * 32 + 32, side]
                        term = jnp.where(block_half == zi % 4, strip, 0.0)
                        total = term if total is None else total + term
                if dz == 0:
                    strip = faces[0:32, half : half + 128]
                    total = total + jnp.where(block_half == (2 * b) % 4, strip, 0.0)
                if dz == 2:
                    strip = faces[224:256, half : half + 128]
                    total = total + jnp.where(block_half == (2 * b + 1) % 4, strip, 0.0)
                total = total + pltpu.roll(total, 64, 1)
                total = total + pltpu.roll(total, 32, 1)
                index = (a * 3 + b) * 3 + dz
                sums[26 - index if reverse else index] = total
    for k in range(7):
        packed = sums[4 * k]
        for j in range(1, 4):
            packed = jnp.where(block_half == j, sums[4 * k + j], packed)
        parts_ref[first_part + 2 * k] = packed[0:16]
        parts_ref[first_part + 2 * k + 1] = packed[16:32]


def step_kernel(
    coarse_ref,
    active_ref,
    links_ref,
    cot_ref,
    up_ref,
    one_ref,
    two_ref,
    fine_ref,
    grad_one_ref,
    grad_two_ref,
    pack_ref,
    y_buf,
    y_sum,
    high_buf,
    high_sum,
    low_buf,
    cot_buf,
    hid_ref,
    hid_buf,
    rep_one,
    rep_two,
    band_one,
    band_two,
    band_back,
    lift_ref,
    lifted_ref,
    win_cot,
    win_lift,
    win_hid,
    parts_ref,
    first_buf,
    near_buf,
    far_buf,
    total_ref,
    send_sems,
    recv_sems,
):
    position = lax.axis_index("space")
    dp = lax.axis_index("dp")
    row, depth = position // 16, position % 16
    low, high = depth % 4, depth // 4
    me = row * 8 + dp

    def wide(step):
        other = (me + step) % 32
        return other, {"space": (other // 8) * 16 + depth, "dp": other % 8}

    def along_y(step):
        other = (row + step) % 4
        return other, {"space": other * 16 + depth, "dp": dp}

    def near(step):
        other = (low + step) % 4
        return other, {"space": row * 16 + high * 4 + other, "dp": dp}

    def far(step):
        other = (high + step) % 4
        return other, {"space": row * 16 + other * 4 + low, "dp": dp}

    after = {"space": (position + 1) % 64, "dp": dp}
    before = {"space": (position + 63) % 64, "dp": dp}

    barrier = pltpu.get_barrier_semaphore()
    for step in range(1, 4):
        pl.semaphore_signal(barrier, inc=1, device_id=near(step)[1], device_id_type=MESH_ID)
        pl.semaphore_signal(barrier, inc=1, device_id=far(step)[1], device_id_type=MESH_ID)
    pl.semaphore_signal(barrier, inc=1, device_id=after, device_id_type=MESH_ID)
    pl.semaphore_signal(barrier, inc=1, device_id=before, device_id_type=MESH_ID)
    for step in range(1, 32):
        pl.semaphore_signal(barrier, inc=1, device_id=wide(step)[1], device_id_type=MESH_ID)

    def send(source, target, device, phase):
        pltpu.make_async_remote_copy(
            src_ref=source,
            dst_ref=target,
            send_sem=send_sems.at[phase],
            recv_sem=recv_sems.at[phase],
            device_id=device,
            device_id_type=MESH_ID,
        ).start()

    def finish(part, phase):
        pltpu.make_async_copy(part, part, recv_sems.at[phase]).wait()

    def sent(part, phase):
        pltpu.make_async_copy(part, part, send_sems.at[phase]).wait()

    pack_ref[...] = picked_rows(active_ref, coarse_ref, position).astype(BF16)
    pl.semaphore_wait(barrier, 39)

    for step in range(1, 4):
        other, device = along_y(step)
        start = pl.multiple_of(other * 128, 128)
        send(pack_ref.at[pl.ds(start, 144)], y_buf.at[row], device, 0)
    send(cot_ref, cot_buf.at[0], after, 3)
    send(cot_ref, cot_buf.at[1], before, 3)
    fill_lift(lift_ref, up_ref)
    rep_two[...] = repeat_weights(two_ref)
    fill_band_back(band_back, rep_two)
    finish(y_buf.at[pl.ds(0, 3)], 0)
    total = pack_ref[pl.ds(pl.multiple_of(row * 128, 128), 144)].astype(F32)
    for step in range(1, 4):
        total = total + y_buf[(row + step) % 4].astype(F32)
    y_sum[...] = total.astype(BF16)
    for step in range(1, 4):
        other, device = far(step)
        start = pl.multiple_of(other * 32, 32)
        send(y_sum.at[pl.ds(start, 48)], high_buf.at[high], device, 1)
    rep_one[...] = repeat_weights(one_ref)
    fill_band(band_one, rep_one)
    finish(high_buf.at[pl.ds(0, 3)], 1)
    total = y_sum[pl.ds(pl.multiple_of(high * 32, 32), 48)].astype(F32)
    for step in range(1, 4):
        total = total + high_buf[(high + step) % 4].astype(F32)
    high_sum[...] = total
    for step in range(1, 4):
        other, device = near(step)
        start = pl.multiple_of(other * 8, 8)
        send(high_sum.at[pl.ds(start, 24)], low_buf.at[low], device, 2)

    finish(cot_buf, 3)

    def cot_before(n):
        return cot_buf[0, n * 64 : n * 64 + 64].astype(F32).reshape(8, 8, 256)

    def cot_own(n):
        return cot_ref[n * 64 : n * 64 + 64].astype(F32).reshape(8, 8, 256)

    def cot_after(n):
        return cot_buf[1, n * 64 : n * 64 + 64].astype(F32).reshape(8, 8, 256)

    fill_windows(win_cot, links_ref, position, cot_before, cot_own, cot_after)
    back = convolve_back(win_cot, band_back)
    finish(low_buf.at[pl.ds(0, 3)], 2)

    rows = high_sum[pl.ds(pl.multiple_of(low * 8, 8), 24)]
    for step in range(1, 4):
        rows = rows + low_buf[(low + step) % 4]
    y_index = iota((8, 128), 0)
    pieces = []
    for j in range(3):
        for a in range(2):
            for n in range(2):
                at = j * 8 + n * 4 + a * 2
                near_half = jnp.broadcast_to(rows[at : at + 1], (8, 128))
                far_half = jnp.broadcast_to(rows[at + 1 : at + 2], (8, 128))
                cell = jnp.where(y_index < 4, near_half, far_half)
                pieces.append(
                    jnp.concatenate(
                        [jnp.where((y_index & 3) == ky, cell, 0.0) for ky in range(4)], axis=1
                    )
                )
    cells = jnp.concatenate(pieces, axis=0).astype(BF16)
    lifted = jnp.dot(cells, lift_ref[...], preferred_element_type=F32).astype(BF16).astype(F32)
    for j in range(3):
        for a in range(2):
            for kx in range(4):
                part = lifted[j * 32 + a * 16 : j * 32 + a * 16 + 16, kx * 256 : kx * 256 + 256]
                lifted_ref[j, a * 4 + kx] = part

    def lifted_of(j):
        return lambda n: lifted_ref[j, :, n * 8 : n * 8 + 8, :]

    fill_windows(win_lift, links_ref, position, lifted_of(0), lifted_of(1), lifted_of(2))
    pre = convolve(win_lift, band_one)
    sigmoid = 1.0 / (1.0 + jnp.exp(-pre))
    hidden = (pre * sigmoid).astype(BF16)
    hid_ref[...] = hidden
    send(hid_ref, hid_buf.at[0], after, 4)
    send(hid_ref, hid_buf.at[1], before, 4)
    grad_pre = (back * sigmoid * (1.0 + pre * (1.0 - sigmoid))).astype(BF16)

    turned_hidden = jnp.transpose(hidden.astype(F32)).astype(BF16)
    turned_grad = jnp.transpose(grad_pre.astype(F32)).astype(BF16)
    weight_products(turned_hidden, win_cot, parts_ref, 14, True)
    weight_products(turned_grad, win_lift, parts_ref, 0, False)
    for k in range(28, 32):
        parts_ref[k] = jnp.zeros((16, 128), F32)

    for step in range(1, 32):
        other, device = wide(step)
        send(parts_ref.at[other], first_buf.at[me], device, 5)
    fill_band(band_two, rep_two)
    finish(first_buf.at[pl.ds(0, 31)], 5)
    first_buf[me] = parts_ref[me]
    near_buf[low] = jnp.sum(first_buf[...], axis=0)
    for step in range(1, 4):
        send(near_buf.at[low], near_buf.at[low], near(step)[1], 6)
    finish(hid_buf, 4)

    def hid_of(ref):
        def part(n):
            return ref[...].astype(F32).reshape(8, 16, 256)[:, n * 8 : n * 8 + 8, :]

        return part

    fill_windows(
        win_hid, links_ref, position, hid_of(hid_buf.at[0]), hid_of(hid_ref), hid_of(hid_buf.at[1])
    )
    finish(near_buf.at[pl.ds(0, 3)], 6)
    far_buf[high] = (near_buf[0] + near_buf[1]) + (near_buf[2] + near_buf[3])
    for step in range(1, 4):
        send(far_buf.at[high], far_buf.at[high], far(step)[1], 7)
    second = convolve(win_hid, band_two)
    scale = 1.0 / math.sqrt(8 * 128 * 512)
    finish(far_buf.at[pl.ds(0, 3)], 7)
    total_ref[me] = ((far_buf[0] + far_buf[1]) + (far_buf[2] + far_buf[3])) * scale
    for step in range(1, 32):
        send(total_ref.at[me], total_ref.at[me], wide(step)[1], 8)
    fine = second.reshape(8, 16, 256) + lifted_ref[1]
    for n in range(2):
        fine_ref[n * 64 : n * 64 + 64] = fine[:, n * 8 : n * 8 + 8, :].reshape(64, 256).astype(BF16)
    finish(total_ref.at[pl.ds(0, 31)], 8)

    for k in range(7):
        packed = total_ref[2 * k : 2 * k + 2].reshape(32, 128)
        turned = jnp.transpose(packed).reshape(4, 32, 32)
        count = min(4, 27 - 4 * k)
        grad_one_ref[4 * k : 4 * k + count] = turned[0:count]
        packed = total_ref[14 + 2 * k : 14 + 2 * k + 2].reshape(32, 128)
        for j in range(count):
            moved = packed if j == 0 else pltpu.roll(packed, 128 - 32 * j, 1)
            grad_two_ref[4 * k + j] = moved[:, 0:32]

    sent(y_buf.at[pl.ds(0, 3)], 0)
    sent(high_buf.at[pl.ds(0, 3)], 1)
    sent(low_buf.at[pl.ds(0, 3)], 2)
    sent(cot_buf, 3)
    sent(hid_buf, 4)
    sent(first_buf.at[pl.ds(0, 31)], 5)
    sent(near_buf.at[pl.ds(0, 3)], 6)
    sent(far_buf.at[pl.ds(0, 3)], 7)
    sent(total_ref.at[pl.ds(0, 31)], 8)


def body(coarse_latents, active_blocks, face_links, cotangent, up_weight, conv_one, conv_two):
    vmem = pl.BlockSpec(memory_space=pltpu.VMEM)
    smem = pl.BlockSpec(memory_space=pltpu.SMEM)
    scratch = [
        ((528, 128), BF16),
        ((4, 144, 128), BF16),
        ((144, 128), BF16),
        ((4, 48, 128), BF16),
        ((48, 128), F32),
        ((4, 24, 128), F32),
        ((2, 128, 256), BF16),
        ((128, 256), BF16),
        ((2, 128, 256), BF16),
        ((864, 256), F32),
        ((864, 256), F32),
        ((3, 1024, 256), BF16),
        ((3, 1024, 256), BF16),
        ((3, 256, 1024), BF16),
        ((512, 1024), BF16),
        ((3, 8, 16, 256), F32),
        ((10, 16, 1024), BF16),
        ((10, 16, 1024), BF16),
        ((10, 16, 1024), BF16),
        ((32, 16, 128), F32),
        ((32, 16, 128), F32),
        ((4, 16, 128), F32),
        ((4, 16, 128), F32),
        ((32, 16, 128), F32),
    ]
    fine, grad_one, grad_two = pl.pallas_call(
        step_kernel,
        out_shape=(
            jax.ShapeDtypeStruct((128, 256), BF16),
            jax.ShapeDtypeStruct((27, 32, 32), F32),
            jax.ShapeDtypeStruct((27, 32, 32), F32),
        ),
        in_specs=[vmem, vmem, smem, vmem, vmem, vmem, vmem],
        out_specs=(vmem, vmem, vmem),
        scratch_shapes=[pltpu.VMEM(*one) for one in scratch]
        + [pltpu.SemaphoreType.DMA((9,)), pltpu.SemaphoreType.DMA((9,))],
        compiler_params=pltpu.CompilerParams(
            collective_id=0, has_side_effects=True, vmem_limit_bytes=40 * 1024 * 1024
        ),
    )(
        coarse_latents[0],
        active_blocks,
        face_links[0],
        cotangent.reshape(128, 256),
        up_weight,
        conv_one.reshape(864, 32),
        conv_two.reshape(864, 32),
    )
    return fine.reshape(1, 2, 8, 8, 256), grad_one, grad_two


def solution(mesh):
    return jax.shard_map(
        body,
        mesh=mesh,
        in_specs=(
            P("dp", "space", None),
            P("dp", None),
            P("dp", "space", None),
            P("dp", "space", None, None, None),
            P(),
            P(),
            P(),
        ),
        out_specs=(P("dp", "space", None, None, None), P(), P()),
        check_vma=False,
    )
```

```python
import math

import jax
import jax.numpy as jnp
from jax import lax
from jax.experimental import pallas as pl
from jax.experimental.pallas import tpu as pltpu
from jax.sharding import PartitionSpec as P

MESH_ID = pl.DeviceIdType.MESH
F32 = jnp.float32
BF16 = jnp.bfloat16


def iota(shape, dim):
    return lax.broadcasted_iota(jnp.int32, shape, dim)


def picked_rows(active_ref, coarse_ref, position):
    rows = 528
    group = ((iota((rows, 128), 0) >> 2) + 126) & 127
    listed = active_ref[...].astype(F32)
    mine = jnp.where(group == iota((rows, 128), 1), listed, 0.0)
    column = jnp.sum(mine, axis=1, keepdims=True)
    local = column - (position * 64).astype(F32)
    quarter = ((iota((rows, 256), 0) & 3) * 64).astype(F32)
    held = (local >= 0.0) & (local < 64.0)
    target = jnp.where(held, local, -1000.0) + quarter
    chosen = jnp.where(iota((rows, 256), 1).astype(F32) == target, 1.0, 0.0).astype(BF16)
    source = jnp.concatenate([coarse_ref[:, k * 128 : (k + 1) * 128] for k in range(4)], axis=0)
    return jnp.dot(chosen, source, preferred_element_type=F32)


def repeat_weights(weight_ref):
    pattern = jnp.where((iota((32, 256), 1) & 31) == iota((32, 256), 0), 1.0, 0.0).astype(BF16)
    return jnp.dot(weight_ref[...], pattern, preferred_element_type=F32)


def fill_band(band_ref, rep_ref):
    block = iota((32, 256), 1) >> 5
    for a in range(3):
        for b in range(3):
            base = (a * 3 + b) * 96
            low = rep_ref[base : base + 32, :]
            mid = rep_ref[base + 32 : base + 64, :]
            high = rep_ref[base + 64 : base + 96, :]
            for zi in range(8):
                strip = jnp.where(block == zi - 1, high, 0.0)
                strip = jnp.where(block == zi, mid, strip)
                strip = jnp.where(block == zi + 1, low, strip)
                first = b * 256 + zi * 32
                band_ref[a, first : first + 32, :] = strip.astype(BF16)
            first = 768 + b * 64
            band_ref[a, first : first + 32, :] = jnp.where(block == 0, low, 0.0).astype(BF16)
            band_ref[a, first + 32 : first + 64, :] = jnp.where(block == 7, high, 0.0).astype(BF16)
        band_ref[a, 960:1024, :] = jnp.zeros((64, 256), BF16)


def fill_band_back(band_ref, rep_ref):
    block = iota((32, 256), 1) >> 5
    for a in range(3):
        faces_first = jnp.zeros((32, 256), F32)
        faces_last = jnp.zeros((32, 256), F32)
        for b in range(3):
            base = ((2 - a) * 3 + 2 - b) * 96
            low = rep_ref[base : base + 32, :]
            mid = rep_ref[base + 32 : base + 64, :]
            high = rep_ref[base + 64 : base + 96, :]
            for zo in range(8):
                strip = jnp.where(block == zo + 1, low, 0.0)
                strip = jnp.where(block == zo, mid, strip)
                strip = jnp.where(block == zo - 1, high, strip)
                band_ref[a, zo * 32 : zo * 32 + 32, b * 256 : b * 256 + 256] = strip.astype(BF16)
            faces_first = jnp.where(block == 2 * b, high, faces_first)
            faces_last = jnp.where(block == 2 * b + 1, low, faces_last)
        band_ref[a, 0:32, 768:1024] = faces_first.astype(BF16)
        band_ref[a, 32:224, 768:1024] = jnp.zeros((192, 256), BF16)
        band_ref[a, 224:256, 768:1024] = faces_last.astype(BF16)


def fill_lift(lift_ref, up_ref):
    lift_ref[...] = jnp.zeros((512, 1024), BF16)
    for ky in range(4):
        for kx in range(4):
            part = up_ref[:, (kx * 4 + ky) * 128 : (kx * 4 + ky + 1) * 128]
            for c in range(2):
                row = ky * 128 + c * 64
                lane = kx * 256 + c * 128
                lift_ref[row : row + 64, lane : lane + 128] = part


def chosen_neighbour(links_ref, position, brick, face, before, own, after):
    link = links_ref[brick, face]
    if face % 2 == 0:
        outer, first = before, jnp.where(position > 0, 2 * position - 2, -8)
    else:
        outer, first = after, 2 * position + 2
    total = None
    for slices, base in ((outer, first), (own, 2 * position)):
        for m in range(2):
            mask = jnp.where(link == base + m, 1.0, 0.0).astype(F32)
            term = slices[m] * mask
            total = term if total is None else total + term
    return total


def fill_windows(win_ref, links_ref, position, before, own, after):
    row = iota((8, 8, 256), 1)
    row_face = iota((8, 256), 0)
    lane = iota((8, 8, 128), 2)
    row_half = iota((8, 8, 128), 1)
    shifted = []
    faces = []
    for n in range(2):
        volume = own(n)

        def neighbour(face, part):
            sources = [[part(f, m) for m in range(2)] for f in (before, own, after)]
            return chosen_neighbour(links_ref, position, n, face, *sources)

        y_minus = neighbour(2, lambda f, m: f(m)[:, 7:8, :])
        y_plus = neighbour(3, lambda f, m: f(m)[:, 0:1, :])
        back_one = jnp.where(row == 0, y_minus, pltpu.roll(volume, 1, 1))
        ahead_one = jnp.where(row == 7, y_plus, pltpu.roll(volume, 7, 1))
        z_minus = neighbour(4, lambda f, m: f(m)[:, :, 128:256])
        z_plus = neighbour(5, lambda f, m: f(m)[:, :, 0:128])
        pair = pltpu.roll(jnp.where(lane >= 64, z_minus, z_plus), 32, 2)
        pair = jnp.where(lane < 64, pair, 0.0)
        first = jnp.where(row_half == 0, 0.0, pltpu.roll(pair, 1, 1)) + pltpu.roll(pair, 64, 2)
        second = jnp.where(row_half == 7, 0.0, pltpu.roll(pair, 7, 1))
        shifted.append((back_one, volume, ahead_one, first, second))
        ends = []
        for face, x in ((0, 7), (1, 0)):
            plane = neighbour(face, lambda f, m: f(m)[x])
            ends.append(
                (
                    jnp.where(row_face == 0, 0.0, pltpu.roll(plane, 1, 0)),
                    plane,
                    jnp.where(row_face == 7, 0.0, pltpu.roll(plane, 7, 0)),
                )
            )
        faces.append(ends)
    for k in range(5):
        both = jnp.concatenate([shifted[0][k], shifted[1][k]], axis=1).astype(BF16)
        first = k * 256 if k < 4 else 896
        win_ref[1:9, :, first : first + both.shape[2]] = both
    for end, x in ((0, 0), (1, 9)):
        for k in range(3):
            both = jnp.concatenate([faces[0][end][k], faces[1][end][k]], axis=0)
            win_ref[x, :, k * 256 : k * 256 + 256] = both.astype(BF16)
        win_ref[x, :, 768:1024] = jnp.zeros((16, 256), BF16)


def window(win_ref, a):
    return win_ref[a : a + 8].reshape(128, 1024)


def convolve(win_ref, band_ref):
    total = None
    for a in range(3):
        term = jnp.dot(window(win_ref, a), band_ref[a], preferred_element_type=F32)
        total = term if total is None else total + term
    return total


def convolve_back(win_ref, band_ref):
    total = None
    for a in range(3):
        term = lax.dot_general(
            window(win_ref, a), band_ref[a], (((1,), (1,)), ((), ())), preferred_element_type=F32
        )
        total = term if total is None else total + term
    return total


def weight_products(turned, win_ref, parts_ref, first_part, reverse):
    block = iota((32, 256), 1) >> 5
    block_half = iota((32, 128), 1) >> 5
    sums = [None] * 28
    sums[27] = jnp.zeros((32, 128), F32)
    for a in range(3):
        seen = window(win_ref, a)
        faces = jnp.dot(turned, seen[:, 768:1024], preferred_element_type=F32)
        for b in range(3):
            outer = jnp.dot(turned, seen[:, b * 256 : b * 256 + 256], preferred_element_type=F32)
            half = (b // 2) * 128
            for dz in range(3):
                total = None
                for z in range(8):
                    zi = z + dz - 1
                    if 0 <= zi < 8:
                        side = slice(0, 128) if zi < 4 else slice(128, 256)
                        strip = outer[z * 32 : z * 32 + 32, side]
                        term = jnp.where(block_half == zi % 4, strip, 0.0)
                        total = term if total is None else total + term
                if dz == 0:
                    strip = faces[0:32, half : half + 128]
                    total = total + jnp.where(block_half == (2 * b) % 4, strip, 0.0)
                if dz == 2:
                    strip = faces[224:256, half : half + 128]
                    total = total + jnp.where(block_half == (2 * b + 1) % 4, strip, 0.0)
                total = total + pltpu.roll(total, 64, 1)
                total = total + pltpu.roll(total, 32, 1)
                index = (a * 3 + b) * 3 + dz
                sums[26 - index if reverse else index] = total
    for k in range(7):
        packed = sums[4 * k]
        for j in range(1, 4):
            packed = jnp.where(block_half == j, sums[4 * k + j], packed)
        parts_ref[first_part + 2 * k] = packed[0:16]
        parts_ref[first_part + 2 * k + 1] = packed[16:32]


def step_kernel(
    coarse_in,
    active_in,
    links_in,
    cot_in,
    up_in,
    one_in,
    two_in,
    fine_ref,
    sums_ref,
    coarse_ref,
    active_ref,
    links_ref,
    cot_ref,
    up_ref,
    one_ref,
    two_ref,
    pack_ref,
    y_buf,
    y_sum,
    cross_buf,
    cross_sum,
    high_buf,
    high_sum,
    low_buf,
    cot_buf,
    hid_ref,
    hid_buf,
    rep_one,
    rep_two,
    band_one,
    band_two,
    band_back,
    lift_ref,
    lifted_ref,
    win_cot,
    win_lift,
    win_hid,
    parts_ref,
    first_buf,
    near_buf,
    far_own,
    far_buf,
    total_ref,
    send_sems,
    recv_sems,
    copy_sems,
):
    position = lax.axis_index("space")
    dp = lax.axis_index("dp")
    row, depth = position // 16, position % 16
    low, high = depth % 4, depth // 4
    me = row * 8 + dp

    def wide(step):
        other = (me + step) % 32
        return other, {"space": (other // 8) * 16 + depth, "dp": other % 8}

    def along_y(step):
        other = (row + step) % 4
        return other, {"space": other * 16 + depth, "dp": dp}

    def near(step):
        other = (low + step) % 4
        return other, {"space": row * 16 + high * 4 + other, "dp": dp}

    def far(other):
        return {"space": row * 16 + other * 4 + low, "dp": dp}

    half, odd = high // 2, high % 2
    across = far(3 - high)
    beside = far(high + 1 - 2 * odd)
    after = {"space": position + 1, "dp": dp}
    before = {"space": position - 1, "dp": dp}
    has_after, has_before = position < 63, position > 0

    barrier = pltpu.get_barrier_semaphore()
    def greet(device):
        pl.semaphore_signal(barrier, inc=1, device_id=device, device_id_type=MESH_ID)

    greet(across)
    greet(beside)

    @pl.when(has_after)
    def _():
        greet(after)

    @pl.when(has_before)
    def _():
        greet(before)

    for step in range(1, 4):
        greet(near(step)[1])
    for step in range(1, 32):
        greet(wide(step)[1])

    sources = (coarse_in, active_in, cot_in, links_in, two_in, up_in, one_in)
    targets = (coarse_ref, active_ref, cot_ref, links_ref, two_ref, up_ref, one_ref)
    fetches = [
        pltpu.make_async_copy(source, target, copy_sems.at[k])
        for k, (source, target) in enumerate(zip(sources, targets))
    ]
    for fetch in fetches:
        fetch.start()

    def send(source, target, device, phase):
        pltpu.make_async_remote_copy(
            src_ref=source,
            dst_ref=target,
            send_sem=send_sems.at[phase],
            recv_sem=recv_sems.at[phase],
            device_id=device,
            device_id_type=MESH_ID,
        ).start()

    def finish(part, phase):
        pltpu.make_async_copy(part, part, recv_sems.at[phase]).wait()

    def sent(part, phase):
        pltpu.make_async_copy(part, part, send_sems.at[phase]).wait()

    fetches[0].wait()
    fetches[1].wait()
    pack_ref[...] = picked_rows(active_ref, coarse_ref, position).astype(BF16)
    fetches[2].wait()
    partners = 36 + jnp.where(has_after, 1, 0) + jnp.where(has_before, 1, 0)
    pl.semaphore_wait(barrier, partners)

    for step in range(1, 4):
        other, device = along_y(step)
        start = pl.multiple_of(other * 128, 128)
        send(pack_ref.at[pl.ds(start, 144)], y_buf.at[row], device, 0)

    @pl.when(has_after)
    def _():
        send(cot_ref, cot_buf.at[0], after, 3)

    @pl.when(has_before)
    def _():
        send(cot_ref, cot_buf.at[1], before, 9)

    for fetch in fetches[3:]:
        fetch.wait()
    fill_lift(lift_ref, up_ref)
    rep_two[...] = repeat_weights(two_ref)
    fill_band_back(band_back, rep_two)
    finish(y_buf.at[pl.ds(0, 3)], 0)
    total = pack_ref[pl.ds(pl.multiple_of(row * 128, 128), 144)].astype(F32)
    for step in range(1, 4):
        total = total + y_buf[(row + step) % 4].astype(F32)
    y_sum[...] = total.astype(BF16)
    send(y_sum.at[pl.ds(pl.multiple_of(64 - half * 64, 64), 80)], cross_buf, across, 1)
    rep_one[...] = repeat_weights(one_ref)
    fill_band(band_one, rep_one)
    finish(cross_buf, 1)
    total = y_sum[pl.ds(pl.multiple_of(half * 64, 64), 80)].astype(F32) + cross_buf[...].astype(F32)
    cross_sum[...] = total.astype(BF16)
    send(cross_sum.at[pl.ds(pl.multiple_of(32 - odd * 32, 32), 48)], high_buf, beside, 10)

    @pl.when(has_before)
    def _():
        finish(cot_buf.at[0], 3)

    @pl.when(jnp.logical_not(has_before))
    def _():
        cot_buf[0] = jnp.zeros((128, 256), BF16)

    @pl.when(has_after)
    def _():
        finish(cot_buf.at[1], 9)

    @pl.when(jnp.logical_not(has_after))
    def _():
        cot_buf[1] = jnp.zeros((128, 256), BF16)

    def cot_before(n):
        return cot_buf[0, n * 64 : n * 64 + 64].astype(F32).reshape(8, 8, 256)

    def cot_own(n):
        return cot_ref[n * 64 : n * 64 + 64].astype(F32).reshape(8, 8, 256)

    def cot_after(n):
        return cot_buf[1, n * 64 : n * 64 + 64].astype(F32).reshape(8, 8, 256)

    fill_windows(win_cot, links_ref, position, cot_before, cot_own, cot_after)
    finish(high_buf, 10)
    kept = cross_sum[pl.ds(pl.multiple_of(odd * 32, 32), 48)].astype(F32)
    high_sum[...] = kept + high_buf[...].astype(F32)
    for step in range(1, 4):
        other, device = near(step)
        start = pl.multiple_of(other * 8, 8)
        send(high_sum.at[pl.ds(start, 24)], low_buf.at[low], device, 2)

    back = convolve_back(win_cot, band_back)
    finish(low_buf.at[pl.ds(0, 3)], 2)

    rows = high_sum[pl.ds(pl.multiple_of(low * 8, 8), 24)]
    for step in range(1, 4):
        rows = rows + low_buf[(low + step) % 4]
    y_index = iota((8, 128), 0)
    pieces = []
    for j in range(3):
        for a in range(2):
            for n in range(2):
                at = j * 8 + n * 4 + a * 2
                near_half = jnp.broadcast_to(rows[at : at + 1], (8, 128))
                far_half = jnp.broadcast_to(rows[at + 1 : at + 2], (8, 128))
                cell = jnp.where(y_index < 4, near_half, far_half)
                pieces.append(
                    jnp.concatenate(
                        [jnp.where((y_index & 3) == ky, cell, 0.0) for ky in range(4)], axis=1
                    )
                )
    cells = jnp.concatenate(pieces, axis=0).astype(BF16)
    lifted = jnp.dot(cells, lift_ref[...], preferred_element_type=F32).astype(BF16).astype(F32)
    for j in range(3):
        for a in range(2):
            for kx in range(4):
                part = lifted[j * 32 + a * 16 : j * 32 + a * 16 + 16, kx * 256 : kx * 256 + 256]
                lifted_ref[j, a * 4 + kx] = part

    def lifted_of(j):
        return lambda n: lifted_ref[j, :, n * 8 : n * 8 + 8, :]

    fill_windows(win_lift, links_ref, position, lifted_of(0), lifted_of(1), lifted_of(2))
    pre = convolve(win_lift, band_one)
    sigmoid = 1.0 / (1.0 + jnp.exp(-pre))
    hidden = (pre * sigmoid).astype(BF16)
    hid_ref[...] = hidden
    grad_pre = (back * sigmoid * (1.0 + pre * (1.0 - sigmoid))).astype(BF16)

    def send_parts(first, last):
        for part in range(first, last):

            @pl.when(part != me)
            def _():
                device = {"space": (part // 8) * 16 + depth, "dp": part % 8}
                send(parts_ref.at[part], first_buf.at[me], device, 5)

    for k in range(28, 32):
        parts_ref[k] = jnp.zeros((16, 128), F32)
    turned_hidden = jnp.transpose(hidden.astype(F32)).astype(BF16)
    weight_products(turned_hidden, win_cot, parts_ref, 14, True)
    send_parts(14, 32)
    turned_grad = jnp.transpose(grad_pre.astype(F32)).astype(BF16)
    weight_products(turned_grad, win_lift, parts_ref, 0, False)
    send_parts(0, 14)

    @pl.when(has_after)
    def _():
        send(hid_ref, hid_buf.at[0], after, 4)

    @pl.when(has_before)
    def _():
        send(hid_ref, hid_buf.at[1], before, 11)

    fill_band(band_two, rep_two)
    finish(first_buf.at[pl.ds(0, 31)], 5)
    first_buf[me] = parts_ref[me]
    near_buf[low] = jnp.sum(first_buf[...], axis=0)
    for step in range(1, 4):
        send(near_buf.at[low], near_buf.at[low], near(step)[1], 6)
    finish(near_buf.at[pl.ds(0, 3)], 6)
    far_own[0] = (near_buf[0] + near_buf[1]) + (near_buf[2] + near_buf[3])
    send(far_own.at[0], far_buf.at[0], across, 7)

    @pl.when(has_before)
    def _():
        finish(hid_buf.at[0], 4)

    @pl.when(jnp.logical_not(has_before))
    def _():
        hid_buf[0] = jnp.zeros((128, 256), BF16)

    @pl.when(has_after)
    def _():
        finish(hid_buf.at[1], 11)

    @pl.when(jnp.logical_not(has_after))
    def _():
        hid_buf[1] = jnp.zeros((128, 256), BF16)

    def hid_of(ref):
        def part(n):
            return ref[...].astype(F32).reshape(8, 16, 256)[:, n * 8 : n * 8 + 8, :]

        return part

    fill_windows(
        win_hid, links_ref, position, hid_of(hid_buf.at[0]), hid_of(hid_ref), hid_of(hid_buf.at[1])
    )
    finish(far_buf.at[0], 7)
    far_own[1] = far_own[0] + far_buf[0]
    send(far_own.at[1], far_buf.at[1], beside, 12)
    second = convolve(win_hid, band_two)
    fine = second.reshape(8, 16, 256) + lifted_ref[1]
    for n in range(2):
        fine_ref[n * 64 : n * 64 + 64] = fine[:, n * 8 : n * 8 + 8, :].reshape(64, 256).astype(BF16)
    scale = 1.0 / math.sqrt(8 * 128 * 512)
    finish(far_buf.at[1], 12)
    total_ref[me] = (far_own[1] + far_buf[1]) * scale
    for step in range(1, 32):
        send(total_ref.at[me], total_ref.at[me], wide(step)[1], 8)
    finish(total_ref.at[pl.ds(0, 31)], 8)

    sums_ref[...] = total_ref[...]

    sent(y_buf.at[pl.ds(0, 3)], 0)
    sent(cross_buf, 1)
    sent(high_buf, 10)
    sent(low_buf.at[pl.ds(0, 3)], 2)

    @pl.when(has_after)
    def _():
        sent(cot_buf.at[0], 3)
        sent(hid_buf.at[0], 4)

    @pl.when(has_before)
    def _():
        sent(cot_buf.at[1], 9)
        sent(hid_buf.at[1], 11)

    sent(first_buf.at[pl.ds(0, 31)], 5)
    sent(near_buf.at[pl.ds(0, 3)], 6)
    sent(far_buf.at[0], 7)
    sent(far_buf.at[1], 12)
    sent(total_ref.at[pl.ds(0, 31)], 8)


def unpack_kernel(sums_ref, given_ref, fine_ref, grad_one_ref, grad_two_ref):
    fine_ref[...] = given_ref[...]
    for k in range(7):
        packed = sums_ref[2 * k : 2 * k + 2].reshape(32, 128)
        turned = jnp.transpose(packed).reshape(4, 32, 32)
        count = min(4, 27 - 4 * k)
        grad_one_ref[4 * k : 4 * k + count] = turned[0:count]
        packed = sums_ref[14 + 2 * k : 14 + 2 * k + 2].reshape(32, 128)
        for j in range(count):
            moved = packed if j == 0 else pltpu.roll(packed, 128 - 32 * j, 1)
            grad_two_ref[4 * k + j] = moved[:, 0:32]


def body(coarse_latents, active_blocks, face_links, cotangent, up_weight, conv_one, conv_two):
    vmem = pl.BlockSpec(memory_space=pltpu.VMEM)
    outside = pl.BlockSpec(memory_space=pl.ANY)
    scratch = [
        ((528, 128), BF16),
        ((4, 144, 128), BF16),
        ((144, 128), BF16),
        ((80, 128), BF16),
        ((80, 128), BF16),
        ((48, 128), BF16),
        ((48, 128), F32),
        ((4, 24, 128), F32),
        ((2, 128, 256), BF16),
        ((128, 256), BF16),
        ((2, 128, 256), BF16),
        ((864, 256), F32),
        ((864, 256), F32),
        ((3, 1024, 256), BF16),
        ((3, 1024, 256), BF16),
        ((3, 256, 1024), BF16),
        ((512, 1024), BF16),
        ((3, 8, 16, 256), F32),
        ((10, 16, 1024), BF16),
        ((10, 16, 1024), BF16),
        ((10, 16, 1024), BF16),
        ((32, 16, 128), F32),
        ((32, 16, 128), F32),
        ((4, 16, 128), F32),
        ((2, 16, 128), F32),
        ((2, 16, 128), F32),
        ((32, 16, 128), F32),
    ]
    inputs = [
        pltpu.VMEM((64, 512), BF16),
        pltpu.VMEM((1, 128), jnp.int32),
        pltpu.SMEM((2, 6), jnp.int32),
        pltpu.VMEM((128, 256), BF16),
        pltpu.VMEM((64, 2048), BF16),
        pltpu.VMEM((864, 32), BF16),
        pltpu.VMEM((864, 32), BF16),
    ]
    out_shape = (
        jax.ShapeDtypeStruct((128, 256), BF16),
        jax.ShapeDtypeStruct((32, 16, 128), F32),
    )
    given, sums = pl.pallas_call(
        step_kernel,
        out_shape=out_shape,
        in_specs=[outside] * 7,
        out_specs=(vmem, vmem),
        scratch_shapes=inputs
        + [pltpu.VMEM(*one) for one in scratch]
        + [pltpu.SemaphoreType.DMA((count,)) for count in (13, 13, 7)],
        compiler_params=pltpu.CompilerParams(
            collective_id=0, has_side_effects=True, vmem_limit_bytes=62 * 1024 * 1024
        ),
    )(
        coarse_latents[0],
        active_blocks,
        face_links[0],
        cotangent.reshape(128, 256),
        up_weight,
        conv_one.reshape(864, 32),
        conv_two.reshape(864, 32),
    )
    fine, grad_one, grad_two = pl.pallas_call(
        unpack_kernel,
        out_shape=(
            jax.ShapeDtypeStruct((128, 256), BF16),
            jax.ShapeDtypeStruct((27, 32, 32), F32),
            jax.ShapeDtypeStruct((27, 32, 32), F32),
        ),
        in_specs=[vmem] * 2,
        out_specs=(vmem,) * 3,
    )(sums, given)
    return fine.reshape(1, 2, 8, 8, 256), grad_one, grad_two


def solution(mesh):
    return jax.shard_map(
        body,
        mesh=mesh,
        in_specs=(
            P("dp", "space", None),
            P("dp", None),
            P("dp", "space", None),
            P("dp", "space", None, None, None),
            P(),
            P(),
            P(),
        ),
        out_specs=(P("dp", "space", None, None, None), P(), P()),
        check_vma=False,
    )
```

```python
import math

import jax
import jax.numpy as jnp
from jax import lax
from jax.experimental import pallas as pl
from jax.experimental.pallas import tpu as pltpu
from jax.sharding import PartitionSpec as P

MESH_ID = pl.DeviceIdType.MESH
F32 = jnp.float32
BF16 = jnp.bfloat16


def iota(shape, dim):
    return lax.broadcasted_iota(jnp.int32, shape, dim)


def picked_rows(active_ref, coarse_ref, position):
    rows = 528
    group = ((iota((rows, 128), 0) >> 2) + 126) & 127
    listed = active_ref[...].astype(F32)
    mine = jnp.where(group == iota((rows, 128), 1), listed, 0.0)
    column = jnp.sum(mine, axis=1, keepdims=True)
    local = column - (position * 64).astype(F32)
    quarter = ((iota((rows, 256), 0) & 3) * 64).astype(F32)
    held = (local >= 0.0) & (local < 64.0)
    target = jnp.where(held, local, -1000.0) + quarter
    chosen = jnp.where(iota((rows, 256), 1).astype(F32) == target, 1.0, 0.0).astype(BF16)
    source = jnp.concatenate([coarse_ref[:, k * 128 : (k + 1) * 128] for k in range(4)], axis=0)
    return jnp.dot(chosen, source, preferred_element_type=F32)


def repeat_weights(weight_ref):
    pattern = jnp.where((iota((32, 256), 1) & 31) == iota((32, 256), 0), 1.0, 0.0).astype(BF16)
    return jnp.dot(weight_ref[...], pattern, preferred_element_type=F32)


def fill_band(band_ref, rep_ref):
    block = iota((32, 256), 1) >> 5
    for a in range(3):
        for b in range(3):
            base = (a * 3 + b) * 96
            low = rep_ref[base : base + 32, :]
            mid = rep_ref[base + 32 : base + 64, :]
            high = rep_ref[base + 64 : base + 96, :]
            for zi in range(8):
                strip = jnp.where(block == zi - 1, high, 0.0)
                strip = jnp.where(block == zi, mid, strip)
                strip = jnp.where(block == zi + 1, low, strip)
                first = b * 256 + zi * 32
                band_ref[a, first : first + 32, :] = strip.astype(BF16)
            first = 768 + b * 64
            band_ref[a, first : first + 32, :] = jnp.where(block == 0, low, 0.0).astype(BF16)
            band_ref[a, first + 32 : first + 64, :] = jnp.where(block == 7, high, 0.0).astype(BF16)
        band_ref[a, 960:1024, :] = jnp.zeros((64, 256), BF16)


def fill_band_back(band_ref, rep_ref):
    block = iota((32, 256), 1) >> 5
    for a in range(3):
        faces_first = jnp.zeros((32, 256), F32)
        faces_last = jnp.zeros((32, 256), F32)
        for b in range(3):
            base = ((2 - a) * 3 + 2 - b) * 96
            low = rep_ref[base : base + 32, :]
            mid = rep_ref[base + 32 : base + 64, :]
            high = rep_ref[base + 64 : base + 96, :]
            for zo in range(8):
                strip = jnp.where(block == zo + 1, low, 0.0)
                strip = jnp.where(block == zo, mid, strip)
                strip = jnp.where(block == zo - 1, high, strip)
                band_ref[a, zo * 32 : zo * 32 + 32, b * 256 : b * 256 + 256] = strip.astype(BF16)
            faces_first = jnp.where(block == 2 * b, high, faces_first)
            faces_last = jnp.where(block == 2 * b + 1, low, faces_last)
        band_ref[a, 0:32, 768:1024] = faces_first.astype(BF16)
        band_ref[a, 32:224, 768:1024] = jnp.zeros((192, 256), BF16)
        band_ref[a, 224:256, 768:1024] = faces_last.astype(BF16)


def fill_lift(lift_ref, up_ref):
    lift_ref[...] = jnp.zeros((512, 1024), BF16)
    for ky in range(4):
        for kx in range(4):
            part = up_ref[:, (kx * 4 + ky) * 128 : (kx * 4 + ky + 1) * 128]
            for c in range(2):
                row = ky * 128 + c * 64
                lane = kx * 256 + c * 128
                lift_ref[row : row + 64, lane : lane + 128] = part


def chosen_neighbour(links_ref, position, brick, face, before, own, after):
    link = links_ref[brick, face]
    if face % 2 == 0:
        outer, first = before, jnp.where(position > 0, 2 * position - 2, -8)
    else:
        outer, first = after, 2 * position + 2
    total = None
    for slices, base in ((outer, first), (own, 2 * position)):
        for m in range(2):
            mask = jnp.where(link == base + m, 1.0, 0.0).astype(F32)
            term = slices[m] * mask
            total = term if total is None else total + term
    return total


def fill_windows(win_ref, links_ref, position, before, own, after):
    row = iota((8, 8, 256), 1)
    row_face = iota((8, 256), 0)
    lane = iota((8, 8, 128), 2)
    row_half = iota((8, 8, 128), 1)
    shifted = []
    faces = []
    for n in range(2):
        volume = own(n)

        def neighbour(face, part):
            sources = [[part(f, m) for m in range(2)] for f in (before, own, after)]
            return chosen_neighbour(links_ref, position, n, face, *sources)

        y_minus = neighbour(2, lambda f, m: f(m)[:, 7:8, :])
        y_plus = neighbour(3, lambda f, m: f(m)[:, 0:1, :])
        back_one = jnp.where(row == 0, y_minus, pltpu.roll(volume, 1, 1))
        ahead_one = jnp.where(row == 7, y_plus, pltpu.roll(volume, 7, 1))
        z_minus = neighbour(4, lambda f, m: f(m)[:, :, 128:256])
        z_plus = neighbour(5, lambda f, m: f(m)[:, :, 0:128])
        pair = pltpu.roll(jnp.where(lane >= 64, z_minus, z_plus), 32, 2)
        pair = jnp.where(lane < 64, pair, 0.0)
        first = jnp.where(row_half == 0, 0.0, pltpu.roll(pair, 1, 1)) + pltpu.roll(pair, 64, 2)
        second = jnp.where(row_half == 7, 0.0, pltpu.roll(pair, 7, 1))
        shifted.append((back_one, volume, ahead_one, first, second))
        ends = []
        for face, x in ((0, 7), (1, 0)):
            plane = neighbour(face, lambda f, m: f(m)[x])
            ends.append(
                (
                    jnp.where(row_face == 0, 0.0, pltpu.roll(plane, 1, 0)),
                    plane,
                    jnp.where(row_face == 7, 0.0, pltpu.roll(plane, 7, 0)),
                )
            )
        faces.append(ends)
    for k in range(5):
        both = jnp.concatenate([shifted[0][k], shifted[1][k]], axis=1).astype(BF16)
        first = k * 256 if k < 4 else 896
        win_ref[1:9, :, first : first + both.shape[2]] = both
    for end, x in ((0, 0), (1, 9)):
        for k in range(3):
            both = jnp.concatenate([faces[0][end][k], faces[1][end][k]], axis=0)
            win_ref[x, :, k * 256 : k * 256 + 256] = both.astype(BF16)
        win_ref[x, :, 768:1024] = jnp.zeros((16, 256), BF16)


def window(win_ref, a):
    return win_ref[a : a + 8].reshape(128, 1024)


def convolve(win_ref, band_ref):
    total = None
    for a in range(3):
        term = jnp.dot(window(win_ref, a), band_ref[a], preferred_element_type=F32)
        total = term if total is None else total + term
    return total


def convolve_back(win_ref, band_ref):
    total = None
    for a in range(3):
        term = lax.dot_general(
            window(win_ref, a), band_ref[a], (((1,), (1,)), ((), ())), preferred_element_type=F32
        )
        total = term if total is None else total + term
    return total


def weight_products(turned, win_ref, parts_ref, first_part, reverse):
    block = iota((32, 256), 1) >> 5
    block_half = iota((32, 128), 1) >> 5
    sums = [None] * 28
    sums[27] = jnp.zeros((32, 128), F32)
    for a in range(3):
        seen = window(win_ref, a)
        faces = jnp.dot(turned, seen[:, 768:1024], preferred_element_type=F32)
        for b in range(3):
            outer = jnp.dot(turned, seen[:, b * 256 : b * 256 + 256], preferred_element_type=F32)
            half = (b // 2) * 128
            for dz in range(3):
                total = None
                for z in range(8):
                    zi = z + dz - 1
                    if 0 <= zi < 8:
                        side = slice(0, 128) if zi < 4 else slice(128, 256)
                        strip = outer[z * 32 : z * 32 + 32, side]
                        term = jnp.where(block_half == zi % 4, strip, 0.0)
                        total = term if total is None else total + term
                if dz == 0:
                    strip = faces[0:32, half : half + 128]
                    total = total + jnp.where(block_half == (2 * b) % 4, strip, 0.0)
                if dz == 2:
                    strip = faces[224:256, half : half + 128]
                    total = total + jnp.where(block_half == (2 * b + 1) % 4, strip, 0.0)
                total = total + pltpu.roll(total, 64, 1)
                total = total + pltpu.roll(total, 32, 1)
                index = (a * 3 + b) * 3 + dz
                sums[26 - index if reverse else index] = total
    for k in range(7):
        packed = sums[4 * k]
        for j in range(1, 4):
            packed = jnp.where(block_half == j, sums[4 * k + j], packed)
        parts_ref[first_part + 2 * k] = packed[0:16]
        parts_ref[first_part + 2 * k + 1] = packed[16:32]


def step_kernel(
    coarse_in,
    active_in,
    links_in,
    cot_in,
    up_in,
    one_in,
    two_in,
    fine_ref,
    sums_ref,
    coarse_ref,
    active_ref,
    links_ref,
    cot_ref,
    up_ref,
    one_ref,
    two_ref,
    pack_ref,
    y_buf,
    y_sum,
    cross_buf,
    cross_sum,
    high_buf,
    high_sum,
    low_buf,
    cot_buf,
    hid_ref,
    hid_buf,
    rep_one,
    rep_two,
    band_one,
    band_two,
    band_back,
    lift_ref,
    lifted_ref,
    win_cot,
    win_lift,
    win_hid,
    parts_ref,
    first_buf,
    near_buf,
    far_buf,
    total_ref,
    send_sems,
    recv_sems,
    copy_sems,
    ready_sem,
):
    position = lax.axis_index("space")
    dp = lax.axis_index("dp")
    row, depth = position // 16, position % 16
    low, high = depth % 4, depth // 4
    me = row * 8 + dp

    def farthest_first():
        for dy in (2, 1, 3, 0):
            for dx in (2, 1, 3, 0):
                for flip in (1, 0):
                    if dy or dx or flip:
                        column = ((dp // 2 + dx) % 4) * 2 + (dp + flip) % 2
                        yield {"space": ((row + dy) % 4) * 16 + depth, "dp": column}

    def along_y(step):
        other = (row + step) % 4
        return other, {"space": other * 16 + depth, "dp": dp}

    def near(step):
        other = (low + step) % 4
        return other, {"space": row * 16 + high * 4 + other, "dp": dp}

    def far(other):
        return {"space": row * 16 + other * 4 + low, "dp": dp}

    half, odd = high // 2, high % 2
    across = far(3 - high)
    beside = far(high + 1 - 2 * odd)
    opposite = far((high + 2) % 4)
    after = {"space": position + 1, "dp": dp}
    before = {"space": position - 1, "dp": dp}
    has_after, has_before = position < 63, position > 0

    barrier = pltpu.get_barrier_semaphore()
    def greet(device):
        pl.semaphore_signal(barrier, inc=1, device_id=device, device_id_type=MESH_ID)

    greet(across)
    greet(beside)

    @pl.when(has_after)
    def _():
        greet(after)

    @pl.when(has_before)
    def _():
        greet(before)

    for step in range(1, 4):
        greet(near(step)[1])
    for device in farthest_first():
        greet(device)

    sources = (coarse_in, active_in, cot_in, links_in, two_in, up_in, one_in)
    targets = (coarse_ref, active_ref, cot_ref, links_ref, two_ref, up_ref, one_ref)
    fetches = [
        pltpu.make_async_copy(source, target, copy_sems.at[k])
        for k, (source, target) in enumerate(zip(sources, targets))
    ]
    for fetch in fetches:
        fetch.start()

    def send(source, target, device, phase):
        pltpu.make_async_remote_copy(
            src_ref=source,
            dst_ref=target,
            send_sem=send_sems.at[phase],
            recv_sem=recv_sems.at[phase],
            device_id=device,
            device_id_type=MESH_ID,
        ).start()

    def finish(part, phase):
        pltpu.make_async_copy(part, part, recv_sems.at[phase]).wait()

    def sent(part, phase):
        pltpu.make_async_copy(part, part, send_sems.at[phase]).wait()

    fetches[0].wait()
    fetches[1].wait()
    pack_ref[...] = picked_rows(active_ref, coarse_ref, position).astype(BF16)
    fetches[2].wait()
    partners = 36 + jnp.where(has_after, 1, 0) + jnp.where(has_before, 1, 0)
    pl.semaphore_wait(barrier, partners)

    for step in range(1, 4):
        other, device = along_y(step)
        start = pl.multiple_of(other * 128, 128)
        send(pack_ref.at[pl.ds(start, 144)], y_buf.at[row], device, 0)

    @pl.when(has_after)
    def _():
        send(cot_ref, cot_buf.at[0], after, 3)

    @pl.when(has_before)
    def _():
        send(cot_ref, cot_buf.at[1], before, 9)

    for fetch in fetches[3:]:
        fetch.wait()
    fill_lift(lift_ref, up_ref)
    rep_two[...] = repeat_weights(two_ref)
    fill_band_back(band_back, rep_two)
    finish(y_buf.at[pl.ds(0, 3)], 0)
    total = pack_ref[pl.ds(pl.multiple_of(row * 128, 128), 144)].astype(F32)
    for step in range(1, 4):
        total = total + y_buf[(row + step) % 4].astype(F32)
    y_sum[...] = total.astype(BF16)
    send(y_sum.at[pl.ds(pl.multiple_of(64 - half * 64, 64), 80)], cross_buf, across, 1)
    rep_one[...] = repeat_weights(one_ref)
    fill_band(band_one, rep_one)
    finish(cross_buf, 1)
    total = y_sum[pl.ds(pl.multiple_of(half * 64, 64), 80)].astype(F32) + cross_buf[...].astype(F32)
    cross_sum[...] = total.astype(BF16)
    send(cross_sum.at[pl.ds(pl.multiple_of(32 - odd * 32, 32), 48)], high_buf, beside, 10)

    @pl.when(has_before)
    def _():
        finish(cot_buf.at[0], 3)

    @pl.when(jnp.logical_not(has_before))
    def _():
        cot_buf[0] = jnp.zeros((128, 256), BF16)

    @pl.when(has_after)
    def _():
        finish(cot_buf.at[1], 9)

    @pl.when(jnp.logical_not(has_after))
    def _():
        cot_buf[1] = jnp.zeros((128, 256), BF16)

    def cot_before(n):
        return cot_buf[0, n * 64 : n * 64 + 64].astype(F32).reshape(8, 8, 256)

    def cot_own(n):
        return cot_ref[n * 64 : n * 64 + 64].astype(F32).reshape(8, 8, 256)

    def cot_after(n):
        return cot_buf[1, n * 64 : n * 64 + 64].astype(F32).reshape(8, 8, 256)

    fill_windows(win_cot, links_ref, position, cot_before, cot_own, cot_after)
    finish(high_buf, 10)
    pl.semaphore_signal(ready_sem, inc=1, device_id=opposite, device_id_type=MESH_ID)
    kept = cross_sum[pl.ds(pl.multiple_of(odd * 32, 32), 48)].astype(F32)
    high_sum[...] = kept + high_buf[...].astype(F32)
    for step in range(1, 4):
        other, device = near(step)
        start = pl.multiple_of(other * 8, 8)
        send(high_sum.at[pl.ds(start, 24)], low_buf.at[low], device, 2)

    back = convolve_back(win_cot, band_back)
    finish(low_buf.at[pl.ds(0, 3)], 2)

    rows = high_sum[pl.ds(pl.multiple_of(low * 8, 8), 24)]
    for step in range(1, 4):
        rows = rows + low_buf[(low + step) % 4]
    y_index = iota((8, 128), 0)
    pieces = []
    for j in range(3):
        for a in range(2):
            for n in range(2):
                at = j * 8 + n * 4 + a * 2
                near_half = jnp.broadcast_to(rows[at : at + 1], (8, 128))
                far_half = jnp.broadcast_to(rows[at + 1 : at + 2], (8, 128))
                cell = jnp.where(y_index < 4, near_half, far_half)
                pieces.append(
                    jnp.concatenate(
                        [jnp.where((y_index & 3) == ky, cell, 0.0) for ky in range(4)], axis=1
                    )
                )
    cells = jnp.concatenate(pieces, axis=0).astype(BF16)
    lifted = jnp.dot(cells, lift_ref[...], preferred_element_type=F32).astype(BF16).astype(F32)
    for j in range(3):
        for a in range(2):
            for kx in range(4):
                part = lifted[j * 32 + a * 16 : j * 32 + a * 16 + 16, kx * 256 : kx * 256 + 256]
                lifted_ref[j, a * 4 + kx] = part

    def lifted_of(j):
        return lambda n: lifted_ref[j, :, n * 8 : n * 8 + 8, :]

    fill_windows(win_lift, links_ref, position, lifted_of(0), lifted_of(1), lifted_of(2))
    pre = convolve(win_lift, band_one)
    sigmoid = 1.0 / (1.0 + jnp.exp(-pre))
    hidden = (pre * sigmoid).astype(BF16)
    hid_ref[...] = hidden
    grad_pre = (back * sigmoid * (1.0 + pre * (1.0 - sigmoid))).astype(BF16)

    def send_parts(first, last):
        for part in range(first, last):

            @pl.when(part != me)
            def _():
                device = {"space": (part // 8) * 16 + depth, "dp": part % 8}
                send(parts_ref.at[part], first_buf.at[me], device, 5)

    for k in range(28, 32):
        parts_ref[k] = jnp.zeros((16, 128), F32)
    turned_hidden = jnp.transpose(hidden.astype(F32)).astype(BF16)
    weight_products(turned_hidden, win_cot, parts_ref, 14, True)
    send_parts(14, 32)
    turned_grad = jnp.transpose(grad_pre.astype(F32)).astype(BF16)
    weight_products(turned_grad, win_lift, parts_ref, 0, False)
    send_parts(0, 14)

    @pl.when(has_after)
    def _():
        send(hid_ref, hid_buf.at[0], after, 4)

    @pl.when(has_before)
    def _():
        send(hid_ref, hid_buf.at[1], before, 11)

    fill_band(band_two, rep_two)
    finish(first_buf.at[pl.ds(0, 31)], 5)
    first_buf[me] = parts_ref[me]
    near_buf[low] = jnp.sum(first_buf[...], axis=0)
    for step in range(1, 4):
        send(near_buf.at[low], near_buf.at[low], near(step)[1], 6)
    finish(near_buf.at[pl.ds(0, 3)], 6)
    far_buf[high] = (near_buf[0] + near_buf[1]) + (near_buf[2] + near_buf[3])
    pl.semaphore_wait(ready_sem, 1)
    for device in (opposite, across, beside):
        send(far_buf.at[high], far_buf.at[high], device, 7)

    @pl.when(has_before)
    def _():
        finish(hid_buf.at[0], 4)

    @pl.when(jnp.logical_not(has_before))
    def _():
        hid_buf[0] = jnp.zeros((128, 256), BF16)

    @pl.when(has_after)
    def _():
        finish(hid_buf.at[1], 11)

    @pl.when(jnp.logical_not(has_after))
    def _():
        hid_buf[1] = jnp.zeros((128, 256), BF16)

    def hid_of(ref):
        def part(n):
            return ref[...].astype(F32).reshape(8, 16, 256)[:, n * 8 : n * 8 + 8, :]

        return part

    fill_windows(
        win_hid, links_ref, position, hid_of(hid_buf.at[0]), hid_of(hid_ref), hid_of(hid_buf.at[1])
    )
    second = convolve(win_hid, band_two)
    fine = second.reshape(8, 16, 256) + lifted_ref[1]
    for n in range(2):
        fine_ref[n * 64 : n * 64 + 64] = fine[:, n * 8 : n * 8 + 8, :].reshape(64, 256).astype(BF16)
    scale = 1.0 / math.sqrt(8 * 128 * 512)
    finish(far_buf.at[pl.ds(0, 3)], 7)
    total_ref[me] = ((far_buf[0] + far_buf[1]) + (far_buf[2] + far_buf[3])) * scale
    for device in farthest_first():
        send(total_ref.at[me], total_ref.at[me], device, 8)
    finish(total_ref.at[pl.ds(0, 31)], 8)

    sums_ref[...] = total_ref[...]

    sent(y_buf.at[pl.ds(0, 3)], 0)
    sent(cross_buf, 1)
    sent(high_buf, 10)
    sent(low_buf.at[pl.ds(0, 3)], 2)

    @pl.when(has_after)
    def _():
        sent(cot_buf.at[0], 3)
        sent(hid_buf.at[0], 4)

    @pl.when(has_before)
    def _():
        sent(cot_buf.at[1], 9)
        sent(hid_buf.at[1], 11)

    sent(first_buf.at[pl.ds(0, 31)], 5)
    sent(near_buf.at[pl.ds(0, 3)], 6)
    sent(far_buf.at[pl.ds(0, 3)], 7)
    sent(total_ref.at[pl.ds(0, 31)], 8)


def unpack_kernel(sums_ref, given_ref, fine_ref, grad_one_ref, grad_two_ref):
    fine_ref[...] = given_ref[...]
    for k in range(7):
        packed = sums_ref[2 * k : 2 * k + 2].reshape(32, 128)
        turned = jnp.transpose(packed).reshape(4, 32, 32)
        count = min(4, 27 - 4 * k)
        grad_one_ref[4 * k : 4 * k + count] = turned[0:count]
        packed = sums_ref[14 + 2 * k : 14 + 2 * k + 2].reshape(32, 128)
        for j in range(count):
            moved = packed if j == 0 else pltpu.roll(packed, 128 - 32 * j, 1)
            grad_two_ref[4 * k + j] = moved[:, 0:32]


def body(coarse_latents, active_blocks, face_links, cotangent, up_weight, conv_one, conv_two):
    vmem = pl.BlockSpec(memory_space=pltpu.VMEM)
    outside = pl.BlockSpec(memory_space=pl.ANY)
    scratch = [
        ((528, 128), BF16),
        ((4, 144, 128), BF16),
        ((144, 128), BF16),
        ((80, 128), BF16),
        ((80, 128), BF16),
        ((48, 128), BF16),
        ((48, 128), F32),
        ((4, 24, 128), F32),
        ((2, 128, 256), BF16),
        ((128, 256), BF16),
        ((2, 128, 256), BF16),
        ((864, 256), F32),
        ((864, 256), F32),
        ((3, 1024, 256), BF16),
        ((3, 1024, 256), BF16),
        ((3, 256, 1024), BF16),
        ((512, 1024), BF16),
        ((3, 8, 16, 256), F32),
        ((10, 16, 1024), BF16),
        ((10, 16, 1024), BF16),
        ((10, 16, 1024), BF16),
        ((32, 16, 128), F32),
        ((32, 16, 128), F32),
        ((4, 16, 128), F32),
        ((4, 16, 128), F32),
        ((32, 16, 128), F32),
    ]
    inputs = [
        pltpu.VMEM((64, 512), BF16),
        pltpu.VMEM((1, 128), jnp.int32),
        pltpu.SMEM((2, 6), jnp.int32),
        pltpu.VMEM((128, 256), BF16),
        pltpu.VMEM((64, 2048), BF16),
        pltpu.VMEM((864, 32), BF16),
        pltpu.VMEM((864, 32), BF16),
    ]
    out_shape = (
        jax.ShapeDtypeStruct((128, 256), BF16),
        jax.ShapeDtypeStruct((32, 16, 128), F32),
    )
    given, sums = pl.pallas_call(
        step_kernel,
        out_shape=out_shape,
        in_specs=[outside] * 7,
        out_specs=(vmem, vmem),
        scratch_shapes=inputs
        + [pltpu.VMEM(*one) for one in scratch]
        + [pltpu.SemaphoreType.DMA((count,)) for count in (13, 13, 7)]
        + [pltpu.SemaphoreType.REGULAR],
        compiler_params=pltpu.CompilerParams(
            collective_id=0, has_side_effects=True, vmem_limit_bytes=62 * 1024 * 1024
        ),
    )(
        coarse_latents[0],
        active_blocks,
        face_links[0],
        cotangent.reshape(128, 256),
        up_weight,
        conv_one.reshape(864, 32),
        conv_two.reshape(864, 32),
    )
    fine, grad_one, grad_two = pl.pallas_call(
        unpack_kernel,
        out_shape=(
            jax.ShapeDtypeStruct((128, 256), BF16),
            jax.ShapeDtypeStruct((27, 32, 32), F32),
            jax.ShapeDtypeStruct((27, 32, 32), F32),
        ),
        in_specs=[vmem] * 2,
        out_specs=(vmem,) * 3,
    )(sums, given)
    return fine.reshape(1, 2, 8, 8, 256), grad_one, grad_two


def solution(mesh):
    return jax.shard_map(
        body,
        mesh=mesh,
        in_specs=(
            P("dp", "space", None),
            P("dp", None),
            P("dp", "space", None),
            P("dp", "space", None, None, None),
            P(),
            P(),
            P(),
        ),
        out_specs=(P("dp", "space", None, None, None), P(), P()),
        check_vma=False,
    )
```

```python
import math

import jax
import jax.numpy as jnp
from jax import lax
from jax.experimental import pallas as pl
from jax.experimental.pallas import tpu as pltpu
from jax.sharding import PartitionSpec as P

MESH_ID = pl.DeviceIdType.MESH
F32 = jnp.float32
BF16 = jnp.bfloat16


def iota(shape, dim):
    return lax.broadcasted_iota(jnp.int32, shape, dim)


def picked_rows(active_ref, coarse_ref, position):
    rows = 528
    group = ((iota((rows, 128), 0) >> 2) + 126) & 127
    listed = active_ref[...].astype(F32)
    mine = jnp.where(group == iota((rows, 128), 1), listed, 0.0)
    column = jnp.sum(mine, axis=1, keepdims=True)
    local = column - (position * 64).astype(F32)
    quarter = ((iota((rows, 256), 0) & 3) * 64).astype(F32)
    held = (local >= 0.0) & (local < 64.0)
    target = jnp.where(held, local, -1000.0) + quarter
    chosen = jnp.where(iota((rows, 256), 1).astype(F32) == target, 1.0, 0.0).astype(BF16)
    source = jnp.concatenate([coarse_ref[:, k * 128 : (k + 1) * 128] for k in range(4)], axis=0)
    return jnp.dot(chosen, source, preferred_element_type=F32)


def repeat_weights(weight_ref):
    pattern = jnp.where((iota((32, 256), 1) & 31) == iota((32, 256), 0), 1.0, 0.0).astype(BF16)
    return jnp.dot(weight_ref[...], pattern, preferred_element_type=F32)


def fill_band(band_ref, rep_ref):
    block = iota((32, 256), 1) >> 5
    for a in range(3):
        for b in range(3):
            base = (a * 3 + b) * 96
            low = rep_ref[base : base + 32, :]
            mid = rep_ref[base + 32 : base + 64, :]
            high = rep_ref[base + 64 : base + 96, :]
            for zi in range(8):
                strip = jnp.where(block == zi - 1, high, 0.0)
                strip = jnp.where(block == zi, mid, strip)
                strip = jnp.where(block == zi + 1, low, strip)
                first = b * 256 + zi * 32
                band_ref[a, first : first + 32, :] = strip.astype(BF16)
            first = 768 + b * 64
            band_ref[a, first : first + 32, :] = jnp.where(block == 0, low, 0.0).astype(BF16)
            band_ref[a, first + 32 : first + 64, :] = jnp.where(block == 7, high, 0.0).astype(BF16)
        band_ref[a, 960:1024, :] = jnp.zeros((64, 256), BF16)


def fill_band_back(band_ref, rep_ref):
    block = iota((32, 256), 1) >> 5
    for a in range(3):
        faces_first = jnp.zeros((32, 256), F32)
        faces_last = jnp.zeros((32, 256), F32)
        for b in range(3):
            base = ((2 - a) * 3 + 2 - b) * 96
            low = rep_ref[base : base + 32, :]
            mid = rep_ref[base + 32 : base + 64, :]
            high = rep_ref[base + 64 : base + 96, :]
            for zo in range(8):
                strip = jnp.where(block == zo + 1, low, 0.0)
                strip = jnp.where(block == zo, mid, strip)
                strip = jnp.where(block == zo - 1, high, strip)
                band_ref[a, zo * 32 : zo * 32 + 32, b * 256 : b * 256 + 256] = strip.astype(BF16)
            faces_first = jnp.where(block == 2 * b, high, faces_first)
            faces_last = jnp.where(block == 2 * b + 1, low, faces_last)
        band_ref[a, 0:32, 768:1024] = faces_first.astype(BF16)
        band_ref[a, 32:224, 768:1024] = jnp.zeros((192, 256), BF16)
        band_ref[a, 224:256, 768:1024] = faces_last.astype(BF16)


def fill_lift(lift_ref, up_ref):
    lift_ref[...] = jnp.zeros((512, 1024), BF16)
    for ky in range(4):
        for kx in range(4):
            part = up_ref[:, (kx * 4 + ky) * 128 : (kx * 4 + ky + 1) * 128]
            for c in range(2):
                row = ky * 128 + c * 64
                lane = kx * 256 + c * 128
                lift_ref[row : row + 64, lane : lane + 128] = part


def chosen_neighbour(links_ref, position, brick, face, before, own, after):
    link = links_ref[brick, face]
    if face % 2 == 0:
        outer, first = before, jnp.where(position > 0, 2 * position - 2, -8)
    else:
        outer, first = after, 2 * position + 2
    total = None
    for slices, base in ((outer, first), (own, 2 * position)):
        for m in range(2):
            mask = jnp.where(link == base + m, 1.0, 0.0).astype(F32)
            term = slices[m] * mask
            total = term if total is None else total + term
    return total


def fill_windows(win_ref, links_ref, position, before, own, after):
    row = iota((8, 8, 256), 1)
    row_face = iota((8, 256), 0)
    lane = iota((8, 8, 128), 2)
    row_half = iota((8, 8, 128), 1)
    shifted = []
    faces = []
    for n in range(2):
        volume = own(n)

        def neighbour(face, part):
            sources = [[part(f, m) for m in range(2)] for f in (before, own, after)]
            return chosen_neighbour(links_ref, position, n, face, *sources)

        y_minus = neighbour(2, lambda f, m: f(m)[:, 7:8, :])
        y_plus = neighbour(3, lambda f, m: f(m)[:, 0:1, :])
        back_one = jnp.where(row == 0, y_minus, pltpu.roll(volume, 1, 1))
        ahead_one = jnp.where(row == 7, y_plus, pltpu.roll(volume, 7, 1))
        z_minus = neighbour(4, lambda f, m: f(m)[:, :, 128:256])
        z_plus = neighbour(5, lambda f, m: f(m)[:, :, 0:128])
        pair = pltpu.roll(jnp.where(lane >= 64, z_minus, z_plus), 32, 2)
        pair = jnp.where(lane < 64, pair, 0.0)
        first = jnp.where(row_half == 0, 0.0, pltpu.roll(pair, 1, 1)) + pltpu.roll(pair, 64, 2)
        second = jnp.where(row_half == 7, 0.0, pltpu.roll(pair, 7, 1))
        shifted.append((back_one, volume, ahead_one, first, second))
        ends = []
        for face, x in ((0, 7), (1, 0)):
            plane = neighbour(face, lambda f, m: f(m)[x])
            ends.append(
                (
                    jnp.where(row_face == 0, 0.0, pltpu.roll(plane, 1, 0)),
                    plane,
                    jnp.where(row_face == 7, 0.0, pltpu.roll(plane, 7, 0)),
                )
            )
        faces.append(ends)
    for k in range(5):
        both = jnp.concatenate([shifted[0][k], shifted[1][k]], axis=1).astype(BF16)
        first = k * 256 if k < 4 else 896
        win_ref[1:9, :, first : first + both.shape[2]] = both
    for end, x in ((0, 0), (1, 9)):
        for k in range(3):
            both = jnp.concatenate([faces[0][end][k], faces[1][end][k]], axis=0)
            win_ref[x, :, k * 256 : k * 256 + 256] = both.astype(BF16)
        win_ref[x, :, 768:1024] = jnp.zeros((16, 256), BF16)


def window(win_ref, a):
    return win_ref[a : a + 8].reshape(128, 1024)


def convolve(win_ref, band_ref):
    total = None
    for a in range(3):
        term = jnp.dot(window(win_ref, a), band_ref[a], preferred_element_type=F32)
        total = term if total is None else total + term
    return total


def convolve_back(win_ref, band_ref):
    total = None
    for a in range(3):
        term = lax.dot_general(
            window(win_ref, a), band_ref[a], (((1,), (1,)), ((), ())), preferred_element_type=F32
        )
        total = term if total is None else total + term
    return total


def weight_products(turned, win_ref, parts_ref, first_part, reverse):
    block = iota((32, 256), 1) >> 5
    block_half = iota((32, 128), 1) >> 5
    sums = [None] * 28
    sums[27] = jnp.zeros((32, 128), F32)
    for a in range(3):
        seen = window(win_ref, a)
        faces = jnp.dot(turned, seen[:, 768:1024], preferred_element_type=F32)
        for b in range(3):
            outer = jnp.dot(turned, seen[:, b * 256 : b * 256 + 256], preferred_element_type=F32)
            half = (b // 2) * 128
            for dz in range(3):
                total = None
                for z in range(8):
                    zi = z + dz - 1
                    if 0 <= zi < 8:
                        side = slice(0, 128) if zi < 4 else slice(128, 256)
                        strip = outer[z * 32 : z * 32 + 32, side]
                        term = jnp.where(block_half == zi % 4, strip, 0.0)
                        total = term if total is None else total + term
                if dz == 0:
                    strip = faces[0:32, half : half + 128]
                    total = total + jnp.where(block_half == (2 * b) % 4, strip, 0.0)
                if dz == 2:
                    strip = faces[224:256, half : half + 128]
                    total = total + jnp.where(block_half == (2 * b + 1) % 4, strip, 0.0)
                total = total + pltpu.roll(total, 64, 1)
                total = total + pltpu.roll(total, 32, 1)
                index = (a * 3 + b) * 3 + dz
                sums[26 - index if reverse else index] = total
    for k in range(7):
        packed = sums[4 * k]
        for j in range(1, 4):
            packed = jnp.where(block_half == j, sums[4 * k + j], packed)
        parts_ref[first_part + 2 * k] = packed[0:16]
        parts_ref[first_part + 2 * k + 1] = packed[16:32]


def step_kernel(
    coarse_in,
    active_in,
    links_in,
    cot_in,
    up_in,
    one_in,
    two_in,
    fine_out,
    sums_ref,
    coarse_ref,
    active_ref,
    links_ref,
    cot_ref,
    up_ref,
    one_ref,
    two_ref,
    pack_ref,
    y_buf,
    y_sum,
    cross_buf,
    cross_sum,
    high_buf,
    high_sum,
    low_buf,
    cot_buf,
    hid_ref,
    hid_buf,
    rep_one,
    rep_two,
    band_one,
    band_two,
    band_back,
    lift_ref,
    lifted_ref,
    win_cot,
    win_lift,
    win_hid,
    parts_ref,
    first_buf,
    near_buf,
    far_buf,
    total_ref,
    send_sems,
    recv_sems,
    copy_sems,
    ready_sem,
    fine_ref,
):
    position = lax.axis_index("space")
    dp = lax.axis_index("dp")
    row, depth = position // 16, position % 16
    low, high = depth % 4, depth // 4
    me = row * 8 + dp

    def farthest_first():
        for dy in (2, 1, 3, 0):
            for dx in (2, 1, 3, 0):
                for flip in (1, 0):
                    if dy or dx or flip:
                        column = ((dp // 2 + dx) % 4) * 2 + (dp + flip) % 2
                        yield {"space": ((row + dy) % 4) * 16 + depth, "dp": column}

    def along_y(step):
        other = (row + step) % 4
        return other, {"space": other * 16 + depth, "dp": dp}

    def near(step):
        other = (low + step) % 4
        return other, {"space": row * 16 + high * 4 + other, "dp": dp}

    def far(other):
        return {"space": row * 16 + other * 4 + low, "dp": dp}

    half, odd = high // 2, high % 2
    across = far(3 - high)
    beside = far(high + 1 - 2 * odd)
    opposite = far((high + 2) % 4)
    after = {"space": position + 1, "dp": dp}
    before = {"space": position - 1, "dp": dp}
    has_after, has_before = position < 63, position > 0

    barrier = pltpu.get_barrier_semaphore()
    def greet(device):
        pl.semaphore_signal(barrier, inc=1, device_id=device, device_id_type=MESH_ID)

    greet(across)
    greet(beside)

    @pl.when(has_after)
    def _():
        greet(after)

    @pl.when(has_before)
    def _():
        greet(before)

    for step in range(1, 4):
        greet(near(step)[1])
    for device in farthest_first():
        greet(device)

    sources = (coarse_in, active_in, cot_in, links_in, two_in, up_in, one_in)
    targets = (coarse_ref, active_ref, cot_ref, links_ref, two_ref, up_ref, one_ref)
    fetches = [
        pltpu.make_async_copy(source, target, copy_sems.at[k])
        for k, (source, target) in enumerate(zip(sources, targets))
    ]
    for fetch in fetches:
        fetch.start()

    def send(source, target, device, phase):
        pltpu.make_async_remote_copy(
            src_ref=source,
            dst_ref=target,
            send_sem=send_sems.at[phase],
            recv_sem=recv_sems.at[phase],
            device_id=device,
            device_id_type=MESH_ID,
        ).start()

    def finish(part, phase):
        pltpu.make_async_copy(part, part, recv_sems.at[phase]).wait()

    def sent(part, phase):
        pltpu.make_async_copy(part, part, send_sems.at[phase]).wait()

    fetches[0].wait()
    fetches[1].wait()
    pack_ref[...] = picked_rows(active_ref, coarse_ref, position).astype(BF16)
    fetches[2].wait()
    partners = 36 + jnp.where(has_after, 1, 0) + jnp.where(has_before, 1, 0)
    pl.semaphore_wait(barrier, partners)

    for step in range(1, 4):
        other, device = along_y(step)
        start = pl.multiple_of(other * 128, 128)
        send(pack_ref.at[pl.ds(start, 144)], y_buf.at[row], device, 0)

    @pl.when(has_after)
    def _():
        send(cot_ref, cot_buf.at[0], after, 3)

    @pl.when(has_before)
    def _():
        send(cot_ref, cot_buf.at[1], before, 9)

    for fetch in fetches[3:]:
        fetch.wait()
    fill_lift(lift_ref, up_ref)
    rep_two[...] = repeat_weights(two_ref)
    fill_band_back(band_back, rep_two)
    finish(y_buf.at[pl.ds(0, 3)], 0)
    total = pack_ref[pl.ds(pl.multiple_of(row * 128, 128), 144)].astype(F32)
    for step in range(1, 4):
        total = total + y_buf[(row + step) % 4].astype(F32)
    y_sum[...] = total.astype(BF16)
    send(y_sum.at[pl.ds(pl.multiple_of(64 - half * 64, 64), 80)], cross_buf, across, 1)
    rep_one[...] = repeat_weights(one_ref)
    fill_band(band_one, rep_one)
    finish(cross_buf, 1)
    total = y_sum[pl.ds(pl.multiple_of(half * 64, 64), 80)].astype(F32) + cross_buf[...].astype(F32)
    cross_sum[...] = total.astype(BF16)
    send(cross_sum.at[pl.ds(pl.multiple_of(32 - odd * 32, 32), 48)], high_buf, beside, 10)

    @pl.when(has_before)
    def _():
        finish(cot_buf.at[0], 3)

    @pl.when(jnp.logical_not(has_before))
    def _():
        cot_buf[0] = jnp.zeros((128, 256), BF16)

    @pl.when(has_after)
    def _():
        finish(cot_buf.at[1], 9)

    @pl.when(jnp.logical_not(has_after))
    def _():
        cot_buf[1] = jnp.zeros((128, 256), BF16)

    def cot_before(n):
        return cot_buf[0, n * 64 : n * 64 + 64].astype(F32).reshape(8, 8, 256)

    def cot_own(n):
        return cot_ref[n * 64 : n * 64 + 64].astype(F32).reshape(8, 8, 256)

    def cot_after(n):
        return cot_buf[1, n * 64 : n * 64 + 64].astype(F32).reshape(8, 8, 256)

    fill_windows(win_cot, links_ref, position, cot_before, cot_own, cot_after)
    finish(high_buf, 10)
    pl.semaphore_signal(ready_sem, inc=1, device_id=opposite, device_id_type=MESH_ID)
    kept = cross_sum[pl.ds(pl.multiple_of(odd * 32, 32), 48)].astype(F32)
    high_sum[...] = kept + high_buf[...].astype(F32)
    for step in range(1, 4):
        other, device = near(step)
        start = pl.multiple_of(other * 8, 8)
        send(high_sum.at[pl.ds(start, 24)], low_buf.at[low], device, 2)

    back = convolve_back(win_cot, band_back)
    finish(low_buf.at[pl.ds(0, 3)], 2)

    rows = high_sum[pl.ds(pl.multiple_of(low * 8, 8), 24)]
    for step in range(1, 4):
        rows = rows + low_buf[(low + step) % 4]
    y_index = iota((8, 128), 0)
    pieces = []
    for j in range(3):
        for a in range(2):
            for n in range(2):
                at = j * 8 + n * 4 + a * 2
                near_half = jnp.broadcast_to(rows[at : at + 1], (8, 128))
                far_half = jnp.broadcast_to(rows[at + 1 : at + 2], (8, 128))
                cell = jnp.where(y_index < 4, near_half, far_half)
                pieces.append(
                    jnp.concatenate(
                        [jnp.where((y_index & 3) == ky, cell, 0.0) for ky in range(4)], axis=1
                    )
                )
    cells = jnp.concatenate(pieces, axis=0).astype(BF16)
    lifted = jnp.dot(cells, lift_ref[...], preferred_element_type=F32).astype(BF16).astype(F32)
    for j in range(3):
        for a in range(2):
            for kx in range(4):
                part = lifted[j * 32 + a * 16 : j * 32 + a * 16 + 16, kx * 256 : kx * 256 + 256]
                lifted_ref[j, a * 4 + kx] = part

    def lifted_of(j):
        return lambda n: lifted_ref[j, :, n * 8 : n * 8 + 8, :]

    fill_windows(win_lift, links_ref, position, lifted_of(0), lifted_of(1), lifted_of(2))
    pre = convolve(win_lift, band_one)
    sigmoid = 1.0 / (1.0 + jnp.exp(-pre))
    hidden = (pre * sigmoid).astype(BF16)
    hid_ref[...] = hidden
    grad_pre = (back * sigmoid * (1.0 + pre * (1.0 - sigmoid))).astype(BF16)

    def send_parts(first, last):
        for part in range(first, last):

            @pl.when(part != me)
            def _():
                device = {"space": (part // 8) * 16 + depth, "dp": part % 8}
                send(parts_ref.at[part], first_buf.at[me], device, 5)

    for k in range(28, 32):
        parts_ref[k] = jnp.zeros((16, 128), F32)
    turned_hidden = jnp.transpose(hidden.astype(F32)).astype(BF16)
    weight_products(turned_hidden, win_cot, parts_ref, 14, True)
    send_parts(14, 32)
    turned_grad = jnp.transpose(grad_pre.astype(F32)).astype(BF16)
    weight_products(turned_grad, win_lift, parts_ref, 0, False)
    send_parts(0, 14)

    @pl.when(has_after)
    def _():
        send(hid_ref, hid_buf.at[0], after, 4)

    @pl.when(has_before)
    def _():
        send(hid_ref, hid_buf.at[1], before, 11)

    fill_band(band_two, rep_two)
    finish(first_buf.at[pl.ds(0, 31)], 5)
    first_buf[me] = parts_ref[me]
    near_buf[low] = jnp.sum(first_buf[...], axis=0)
    for step in range(1, 4):
        send(near_buf.at[low], near_buf.at[low], near(step)[1], 6)
    finish(near_buf.at[pl.ds(0, 3)], 6)
    far_buf[high] = (near_buf[0] + near_buf[1]) + (near_buf[2] + near_buf[3])
    pl.semaphore_wait(ready_sem, 1)
    for device in (opposite, across, beside):
        send(far_buf.at[high], far_buf.at[high], device, 7)

    @pl.when(has_before)
    def _():
        finish(hid_buf.at[0], 4)

    @pl.when(jnp.logical_not(has_before))
    def _():
        hid_buf[0] = jnp.zeros((128, 256), BF16)

    @pl.when(has_after)
    def _():
        finish(hid_buf.at[1], 11)

    @pl.when(jnp.logical_not(has_after))
    def _():
        hid_buf[1] = jnp.zeros((128, 256), BF16)

    def hid_of(ref):
        def part(n):
            return ref[...].astype(F32).reshape(8, 16, 256)[:, n * 8 : n * 8 + 8, :]

        return part

    fill_windows(
        win_hid, links_ref, position, hid_of(hid_buf.at[0]), hid_of(hid_ref), hid_of(hid_buf.at[1])
    )
    second = convolve(win_hid, band_two)
    fine = second.reshape(8, 16, 256) + lifted_ref[1]
    for n in range(2):
        fine_ref[n * 64 : n * 64 + 64] = fine[:, n * 8 : n * 8 + 8, :].reshape(64, 256).astype(BF16)
    fine_copy = pltpu.make_async_copy(fine_ref, fine_out, copy_sems.at[7])
    fine_copy.start()
    scale = 1.0 / math.sqrt(8 * 128 * 512)
    finish(far_buf.at[pl.ds(0, 3)], 7)
    total_ref[me] = ((far_buf[0] + far_buf[1]) + (far_buf[2] + far_buf[3])) * scale
    for device in farthest_first():
        send(total_ref.at[me], total_ref.at[me], device, 8)
    finish(total_ref.at[pl.ds(0, 31)], 8)

    sums_ref[...] = total_ref[...]
    fine_copy.wait()

    sent(y_buf.at[pl.ds(0, 3)], 0)
    sent(cross_buf, 1)
    sent(high_buf, 10)
    sent(low_buf.at[pl.ds(0, 3)], 2)

    @pl.when(has_after)
    def _():
        sent(cot_buf.at[0], 3)
        sent(hid_buf.at[0], 4)

    @pl.when(has_before)
    def _():
        sent(cot_buf.at[1], 9)
        sent(hid_buf.at[1], 11)

    sent(first_buf.at[pl.ds(0, 31)], 5)
    sent(near_buf.at[pl.ds(0, 3)], 6)
    sent(far_buf.at[pl.ds(0, 3)], 7)
    sent(total_ref.at[pl.ds(0, 31)], 8)


def unpack_kernel(sums_ref, given_ref, fine_ref, grad_one_ref, grad_two_ref, sem):
    fine_copy = pltpu.make_async_copy(given_ref, fine_ref, sem)
    fine_copy.start()
    for k in range(7):
        packed = sums_ref[2 * k : 2 * k + 2].reshape(32, 128)
        turned = jnp.transpose(packed).reshape(4, 32, 32)
        count = min(4, 27 - 4 * k)
        grad_one_ref[4 * k : 4 * k + count] = turned[0:count]
        packed = sums_ref[14 + 2 * k : 14 + 2 * k + 2].reshape(32, 128)
        for j in range(count):
            moved = packed if j == 0 else pltpu.roll(packed, 128 - 32 * j, 1)
            grad_two_ref[4 * k + j] = moved[:, 0:32]
    fine_copy.wait()


def body(coarse_latents, active_blocks, face_links, cotangent, up_weight, conv_one, conv_two):
    vmem = pl.BlockSpec(memory_space=pltpu.VMEM)
    outside = pl.BlockSpec(memory_space=pl.ANY)
    scratch = [
        ((528, 128), BF16),
        ((4, 144, 128), BF16),
        ((144, 128), BF16),
        ((80, 128), BF16),
        ((80, 128), BF16),
        ((48, 128), BF16),
        ((48, 128), F32),
        ((4, 24, 128), F32),
        ((2, 128, 256), BF16),
        ((128, 256), BF16),
        ((2, 128, 256), BF16),
        ((864, 256), F32),
        ((864, 256), F32),
        ((3, 1024, 256), BF16),
        ((3, 1024, 256), BF16),
        ((3, 256, 1024), BF16),
        ((512, 1024), BF16),
        ((3, 8, 16, 256), F32),
        ((10, 16, 1024), BF16),
        ((10, 16, 1024), BF16),
        ((10, 16, 1024), BF16),
        ((32, 16, 128), F32),
        ((32, 16, 128), F32),
        ((4, 16, 128), F32),
        ((4, 16, 128), F32),
        ((32, 16, 128), F32),
    ]
    inputs = [
        pltpu.VMEM((64, 512), BF16),
        pltpu.VMEM((1, 128), jnp.int32),
        pltpu.SMEM((2, 6), jnp.int32),
        pltpu.VMEM((128, 256), BF16),
        pltpu.VMEM((64, 2048), BF16),
        pltpu.VMEM((864, 32), BF16),
        pltpu.VMEM((864, 32), BF16),
    ]
    out_shape = (
        jax.ShapeDtypeStruct((128, 256), BF16),
        jax.ShapeDtypeStruct((32, 16, 128), F32),
    )
    given, sums = pl.pallas_call(
        step_kernel,
        out_shape=out_shape,
        in_specs=[outside] * 7,
        out_specs=(outside, vmem),
        scratch_shapes=inputs
        + [pltpu.VMEM(*one) for one in scratch]
        + [pltpu.SemaphoreType.DMA((count,)) for count in (13, 13, 8)]
        + [pltpu.SemaphoreType.REGULAR, pltpu.VMEM((128, 256), BF16)],
        compiler_params=pltpu.CompilerParams(
            collective_id=0, has_side_effects=True, vmem_limit_bytes=62 * 1024 * 1024
        ),
    )(
        coarse_latents[0],
        active_blocks,
        face_links[0],
        cotangent.reshape(128, 256),
        up_weight,
        conv_one.reshape(864, 32),
        conv_two.reshape(864, 32),
    )
    fine, grad_one, grad_two = pl.pallas_call(
        unpack_kernel,
        out_shape=(
            jax.ShapeDtypeStruct((128, 256), BF16),
            jax.ShapeDtypeStruct((27, 32, 32), F32),
            jax.ShapeDtypeStruct((27, 32, 32), F32),
        ),
        in_specs=[vmem, outside],
        out_specs=(outside, vmem, vmem),
        scratch_shapes=[pltpu.SemaphoreType.DMA(())],
    )(sums, given)
    return fine.reshape(1, 2, 8, 8, 256), grad_one, grad_two


def solution(mesh):
    return jax.shard_map(
        body,
        mesh=mesh,
        in_specs=(
            P("dp", "space", None),
            P("dp", None),
            P("dp", "space", None),
            P("dp", "space", None, None, None),
            P(),
            P(),
            P(),
        ),
        out_specs=(P("dp", "space", None, None, None), P(), P()),
        check_vma=False,
    )
```

```python
import math

import jax
import jax.numpy as jnp
from jax import lax
from jax.experimental import pallas as pl
from jax.experimental.pallas import tpu as pltpu
from jax.sharding import PartitionSpec as P

MESH_ID = pl.DeviceIdType.MESH
F32 = jnp.float32
BF16 = jnp.bfloat16


def iota(shape, dim):
    return lax.broadcasted_iota(jnp.int32, shape, dim)


def picked_rows(active_ref, coarse_ref, position):
    rows = 528
    group = ((iota((rows, 128), 0) >> 2) + 126) & 127
    listed = active_ref[...].astype(F32)
    mine = jnp.where(group == iota((rows, 128), 1), listed, 0.0)
    column = jnp.sum(mine, axis=1, keepdims=True)
    local = column - (position * 64).astype(F32)
    quarter = ((iota((rows, 256), 0) & 3) * 64).astype(F32)
    held = (local >= 0.0) & (local < 64.0)
    target = jnp.where(held, local, -1000.0) + quarter
    chosen = jnp.where(iota((rows, 256), 1).astype(F32) == target, 1.0, 0.0).astype(BF16)
    source = jnp.concatenate([coarse_ref[:, k * 128 : (k + 1) * 128] for k in range(4)], axis=0)
    return jnp.dot(chosen, source, preferred_element_type=F32)


def repeat_weights(weight_ref):
    pattern = jnp.where((iota((32, 256), 1) & 31) == iota((32, 256), 0), 1.0, 0.0).astype(BF16)
    return jnp.dot(weight_ref[...], pattern, preferred_element_type=F32)


def fill_band(band_ref, rep_ref):
    block = iota((32, 256), 1) >> 5
    for a in range(3):
        for b in range(3):
            base = (a * 3 + b) * 96
            low = rep_ref[base : base + 32, :]
            mid = rep_ref[base + 32 : base + 64, :]
            high = rep_ref[base + 64 : base + 96, :]
            for zi in range(8):
                strip = jnp.where(block == zi - 1, high, 0.0)
                strip = jnp.where(block == zi, mid, strip)
                strip = jnp.where(block == zi + 1, low, strip)
                first = b * 256 + zi * 32
                band_ref[a, first : first + 32, :] = strip.astype(BF16)
            first = 768 + b * 64
            band_ref[a, first : first + 32, :] = jnp.where(block == 0, low, 0.0).astype(BF16)
            band_ref[a, first + 32 : first + 64, :] = jnp.where(block == 7, high, 0.0).astype(BF16)
        band_ref[a, 960:1024, :] = jnp.zeros((64, 256), BF16)


def fill_band_back(band_ref, rep_ref):
    block = iota((32, 256), 1) >> 5
    for a in range(3):
        faces_first = jnp.zeros((32, 256), F32)
        faces_last = jnp.zeros((32, 256), F32)
        for b in range(3):
            base = ((2 - a) * 3 + 2 - b) * 96
            low = rep_ref[base : base + 32, :]
            mid = rep_ref[base + 32 : base + 64, :]
            high = rep_ref[base + 64 : base + 96, :]
            for zo in range(8):
                strip = jnp.where(block == zo + 1, low, 0.0)
                strip = jnp.where(block == zo, mid, strip)
                strip = jnp.where(block == zo - 1, high, strip)
                band_ref[a, zo * 32 : zo * 32 + 32, b * 256 : b * 256 + 256] = strip.astype(BF16)
            faces_first = jnp.where(block == 2 * b, high, faces_first)
            faces_last = jnp.where(block == 2 * b + 1, low, faces_last)
        band_ref[a, 0:32, 768:1024] = faces_first.astype(BF16)
        band_ref[a, 32:224, 768:1024] = jnp.zeros((192, 256), BF16)
        band_ref[a, 224:256, 768:1024] = faces_last.astype(BF16)


def fill_lift(lift_ref, up_ref):
    lift_ref[...] = jnp.zeros((512, 1024), BF16)
    for ky in range(4):
        for kx in range(4):
            part = up_ref[:, (kx * 4 + ky) * 128 : (kx * 4 + ky + 1) * 128]
            for c in range(2):
                row = ky * 128 + c * 64
                lane = kx * 256 + c * 128
                lift_ref[row : row + 64, lane : lane + 128] = part


def chosen_neighbour(links_ref, position, brick, face, before, own, after):
    link = links_ref[brick, face]
    if face % 2 == 0:
        outer, first = before, jnp.where(position > 0, 2 * position - 2, -8)
    else:
        outer, first = after, 2 * position + 2
    total = None
    for slices, base in ((outer, first), (own, 2 * position)):
        for m in range(2):
            mask = jnp.where(link == base + m, 1.0, 0.0).astype(F32)
            term = slices[m] * mask
            total = term if total is None else total + term
    return total


def fill_windows(win_ref, links_ref, position, before, own, after):
    row = iota((8, 8, 256), 1)
    row_face = iota((8, 256), 0)
    lane = iota((8, 8, 128), 2)
    row_half = iota((8, 8, 128), 1)
    shifted = []
    faces = []
    for n in range(2):
        volume = own(n)

        def neighbour(face, part):
            sources = [[part(f, m) for m in range(2)] for f in (before, own, after)]
            return chosen_neighbour(links_ref, position, n, face, *sources)

        y_minus = neighbour(2, lambda f, m: f(m)[:, 7:8, :])
        y_plus = neighbour(3, lambda f, m: f(m)[:, 0:1, :])
        back_one = jnp.where(row == 0, y_minus, pltpu.roll(volume, 1, 1))
        ahead_one = jnp.where(row == 7, y_plus, pltpu.roll(volume, 7, 1))
        z_minus = neighbour(4, lambda f, m: f(m)[:, :, 128:256])
        z_plus = neighbour(5, lambda f, m: f(m)[:, :, 0:128])
        pair = pltpu.roll(jnp.where(lane >= 64, z_minus, z_plus), 32, 2)
        pair = jnp.where(lane < 64, pair, 0.0)
        first = jnp.where(row_half == 0, 0.0, pltpu.roll(pair, 1, 1)) + pltpu.roll(pair, 64, 2)
        second = jnp.where(row_half == 7, 0.0, pltpu.roll(pair, 7, 1))
        shifted.append((back_one, volume, ahead_one, first, second))
        ends = []
        for face, x in ((0, 7), (1, 0)):
            plane = neighbour(face, lambda f, m: f(m)[x])
            ends.append(
                (
                    jnp.where(row_face == 0, 0.0, pltpu.roll(plane, 1, 0)),
                    plane,
                    jnp.where(row_face == 7, 0.0, pltpu.roll(plane, 7, 0)),
                )
            )
        faces.append(ends)
    for k in range(5):
        both = jnp.concatenate([shifted[0][k], shifted[1][k]], axis=1).astype(BF16)
        first = k * 256 if k < 4 else 896
        win_ref[1:9, :, first : first + both.shape[2]] = both
    for end, x in ((0, 0), (1, 9)):
        for k in range(3):
            both = jnp.concatenate([faces[0][end][k], faces[1][end][k]], axis=0)
            win_ref[x, :, k * 256 : k * 256 + 256] = both.astype(BF16)
        win_ref[x, :, 768:1024] = jnp.zeros((16, 256), BF16)


def window(win_ref, a):
    return win_ref[a : a + 8].reshape(128, 1024)


def convolve(win_ref, band_ref):
    total = None
    for a in range(3):
        term = jnp.dot(window(win_ref, a), band_ref[a], preferred_element_type=F32)
        total = term if total is None else total + term
    return total


def convolve_back(win_ref, band_ref):
    total = None
    for a in range(3):
        term = lax.dot_general(
            window(win_ref, a), band_ref[a], (((1,), (1,)), ((), ())), preferred_element_type=F32
        )
        total = term if total is None else total + term
    return total


def weight_products(turned, win_ref, parts_ref, first_part, reverse):
    block = iota((32, 256), 1) >> 5
    block_half = iota((32, 128), 1) >> 5
    sums = [None] * 28
    sums[27] = jnp.zeros((32, 128), F32)
    for a in range(3):
        seen = window(win_ref, a)
        faces = jnp.dot(turned, seen[:, 768:1024], preferred_element_type=F32)
        for b in range(3):
            outer = jnp.dot(turned, seen[:, b * 256 : b * 256 + 256], preferred_element_type=F32)
            half = (b // 2) * 128
            for dz in range(3):
                total = None
                for z in range(8):
                    zi = z + dz - 1
                    if 0 <= zi < 8:
                        side = slice(0, 128) if zi < 4 else slice(128, 256)
                        strip = outer[z * 32 : z * 32 + 32, side]
                        term = jnp.where(block_half == zi % 4, strip, 0.0)
                        total = term if total is None else total + term
                if dz == 0:
                    strip = faces[0:32, half : half + 128]
                    total = total + jnp.where(block_half == (2 * b) % 4, strip, 0.0)
                if dz == 2:
                    strip = faces[224:256, half : half + 128]
                    total = total + jnp.where(block_half == (2 * b + 1) % 4, strip, 0.0)
                total = total + pltpu.roll(total, 64, 1)
                total = total + pltpu.roll(total, 32, 1)
                index = (a * 3 + b) * 3 + dz
                sums[26 - index if reverse else index] = total
    for k in range(7):
        packed = sums[4 * k]
        for j in range(1, 4):
            packed = jnp.where(block_half == j, sums[4 * k + j], packed)
        parts_ref[first_part + 2 * k] = packed[0:16]
        parts_ref[first_part + 2 * k + 1] = packed[16:32]


def step_kernel(
    coarse_in,
    active_in,
    links_in,
    cot_in,
    up_in,
    one_in,
    two_in,
    fine_ref,
    sums_ref,
    coarse_ref,
    active_ref,
    links_ref,
    cot_ref,
    up_ref,
    one_ref,
    two_ref,
    pack_ref,
    y_buf,
    y_sum,
    cross_buf,
    cross_sum,
    high_buf,
    high_sum,
    low_buf,
    cot_buf,
    hid_ref,
    hid_buf,
    rep_one,
    rep_two,
    band_one,
    band_two,
    band_back,
    lift_ref,
    lifted_ref,
    win_cot,
    win_lift,
    win_hid,
    parts_ref,
    first_buf,
    near_buf,
    far_buf,
    total_ref,
    send_sems,
    recv_sems,
    copy_sems,
    ready_sem,
):
    position = lax.axis_index("space")
    dp = lax.axis_index("dp")
    row, depth = position // 16, position % 16
    low, high = depth % 4, depth // 4
    me = row * 8 + dp

    def farthest_first():
        for dy in (2, 1, 3, 0):
            for dx in (2, 1, 3, 0):
                for flip in (1, 0):
                    if dy or dx or flip:
                        column = ((dp // 2 + dx) % 4) * 2 + (dp + flip) % 2
                        yield {"space": ((row + dy) % 4) * 16 + depth, "dp": column}

    def along_y(step):
        other = (row + step) % 4
        return other, {"space": other * 16 + depth, "dp": dp}

    def near(step):
        other = (low + step) % 4
        return other, {"space": row * 16 + high * 4 + other, "dp": dp}

    def far(other):
        return {"space": row * 16 + other * 4 + low, "dp": dp}

    half, odd = high // 2, high % 2
    across = far(3 - high)
    beside = far(high + 1 - 2 * odd)
    opposite = far((high + 2) % 4)
    after = {"space": position + 1, "dp": dp}
    before = {"space": position - 1, "dp": dp}
    has_after, has_before = position < 63, position > 0

    barrier = pltpu.get_barrier_semaphore()
    def greet(device):
        pl.semaphore_signal(barrier, inc=1, device_id=device, device_id_type=MESH_ID)

    greet(across)
    greet(beside)

    @pl.when(has_after)
    def _():
        greet(after)

    @pl.when(has_before)
    def _():
        greet(before)

    for step in range(1, 4):
        greet(near(step)[1])
    for device in farthest_first():
        greet(device)

    sources = (coarse_in, active_in, cot_in, links_in, two_in, up_in, one_in)
    targets = (coarse_ref, active_ref, cot_ref, links_ref, two_ref, up_ref, one_ref)
    fetches = [
        pltpu.make_async_copy(source, target, copy_sems.at[k])
        for k, (source, target) in enumerate(zip(sources, targets))
    ]
    for fetch in fetches:
        fetch.start()

    def send(source, target, device, phase):
        pltpu.make_async_remote_copy(
            src_ref=source,
            dst_ref=target,
            send_sem=send_sems.at[phase],
            recv_sem=recv_sems.at[phase],
            device_id=device,
            device_id_type=MESH_ID,
        ).start()

    def finish(part, phase):
        pltpu.make_async_copy(part, part, recv_sems.at[phase]).wait()

    def sent(part, phase):
        pltpu.make_async_copy(part, part, send_sems.at[phase]).wait()

    fetches[0].wait()
    fetches[1].wait()
    pack_ref[...] = picked_rows(active_ref, coarse_ref, position).astype(BF16)
    fetches[2].wait()
    partners = 36 + jnp.where(has_after, 1, 0) + jnp.where(has_before, 1, 0)
    pl.semaphore_wait(barrier, partners)

    for step in range(1, 4):
        other, device = along_y(step)
        start = pl.multiple_of(other * 128, 128)
        send(pack_ref.at[pl.ds(start, 144)], y_buf.at[row], device, 0)

    @pl.when(has_after)
    def _():
        send(cot_ref, cot_buf.at[0], after, 3)

    @pl.when(has_before)
    def _():
        send(cot_ref, cot_buf.at[1], before, 9)

    for fetch in fetches[3:]:
        fetch.wait()
    fill_lift(lift_ref, up_ref)
    rep_two[...] = repeat_weights(two_ref)
    fill_band_back(band_back, rep_two)
    finish(y_buf.at[pl.ds(0, 3)], 0)
    total = pack_ref[pl.ds(pl.multiple_of(row * 128, 128), 144)].astype(F32)
    for step in range(1, 4):
        total = total + y_buf[(row + step) % 4].astype(F32)
    y_sum[...] = total.astype(BF16)
    send(y_sum.at[pl.ds(pl.multiple_of(64 - half * 64, 64), 80)], cross_buf, across, 1)
    rep_one[...] = repeat_weights(one_ref)
    fill_band(band_one, rep_one)
    finish(cross_buf, 1)
    total = y_sum[pl.ds(pl.multiple_of(half * 64, 64), 80)].astype(F32) + cross_buf[...].astype(F32)
    cross_sum[...] = total.astype(BF16)
    send(cross_sum.at[pl.ds(pl.multiple_of(32 - odd * 32, 32), 48)], high_buf, beside, 10)

    @pl.when(has_before)
    def _():
        finish(cot_buf.at[0], 3)

    @pl.when(jnp.logical_not(has_before))
    def _():
        cot_buf[0] = jnp.zeros((128, 256), BF16)

    @pl.when(has_after)
    def _():
        finish(cot_buf.at[1], 9)

    @pl.when(jnp.logical_not(has_after))
    def _():
        cot_buf[1] = jnp.zeros((128, 256), BF16)

    def cot_before(n):
        return cot_buf[0, n * 64 : n * 64 + 64].astype(F32).reshape(8, 8, 256)

    def cot_own(n):
        return cot_ref[n * 64 : n * 64 + 64].astype(F32).reshape(8, 8, 256)

    def cot_after(n):
        return cot_buf[1, n * 64 : n * 64 + 64].astype(F32).reshape(8, 8, 256)

    fill_windows(win_cot, links_ref, position, cot_before, cot_own, cot_after)
    finish(high_buf, 10)
    pl.semaphore_signal(ready_sem, inc=1, device_id=opposite, device_id_type=MESH_ID)
    kept = cross_sum[pl.ds(pl.multiple_of(odd * 32, 32), 48)].astype(F32)
    high_sum[...] = kept + high_buf[...].astype(F32)
    for step in range(1, 4):
        other, device = near(step)
        start = pl.multiple_of(other * 8, 8)
        send(high_sum.at[pl.ds(start, 24)], low_buf.at[low], device, 2)

    back = convolve_back(win_cot, band_back)
    finish(low_buf.at[pl.ds(0, 3)], 2)

    rows = high_sum[pl.ds(pl.multiple_of(low * 8, 8), 24)]
    for step in range(1, 4):
        rows = rows + low_buf[(low + step) % 4]
    y_index = iota((8, 128), 0)
    pieces = []
    for j in range(3):
        for a in range(2):
            for n in range(2):
                at = j * 8 + n * 4 + a * 2
                near_half = jnp.broadcast_to(rows[at : at + 1], (8, 128))
                far_half = jnp.broadcast_to(rows[at + 1 : at + 2], (8, 128))
                cell = jnp.where(y_index < 4, near_half, far_half)
                pieces.append(
                    jnp.concatenate(
                        [jnp.where((y_index & 3) == ky, cell, 0.0) for ky in range(4)], axis=1
                    )
                )
    cells = jnp.concatenate(pieces, axis=0).astype(BF16)
    lifted = jnp.dot(cells, lift_ref[...], preferred_element_type=F32).astype(BF16).astype(F32)
    for j in range(3):
        for a in range(2):
            for kx in range(4):
                part = lifted[j * 32 + a * 16 : j * 32 + a * 16 + 16, kx * 256 : kx * 256 + 256]
                lifted_ref[j, a * 4 + kx] = part

    def lifted_of(j):
        return lambda n: lifted_ref[j, :, n * 8 : n * 8 + 8, :]

    fill_windows(win_lift, links_ref, position, lifted_of(0), lifted_of(1), lifted_of(2))
    pre = convolve(win_lift, band_one)
    sigmoid = 1.0 / (1.0 + jnp.exp(-pre))
    hidden = (pre * sigmoid).astype(BF16)
    hid_ref[...] = hidden
    grad_pre = (back * sigmoid * (1.0 + pre * (1.0 - sigmoid))).astype(BF16)

    def send_parts(first, last):
        for part in range(first, last):

            @pl.when(part != me)
            def _():
                device = {"space": (part // 8) * 16 + depth, "dp": part % 8}
                send(parts_ref.at[part], first_buf.at[me], device, 5)

    for k in range(28, 32):
        parts_ref[k] = jnp.zeros((16, 128), F32)
    turned_hidden = jnp.transpose(hidden.astype(F32)).astype(BF16)
    weight_products(turned_hidden, win_cot, parts_ref, 14, True)
    send_parts(14, 32)
    turned_grad = jnp.transpose(grad_pre.astype(F32)).astype(BF16)
    weight_products(turned_grad, win_lift, parts_ref, 0, False)
    send_parts(0, 14)
    fill_band(band_two, rep_two)
    finish(first_buf.at[pl.ds(0, 31)], 5)
    first_buf[me] = parts_ref[me]
    near_buf[low] = jnp.sum(first_buf[...], axis=0)
    for step in range(1, 4):
        send(near_buf.at[low], near_buf.at[low], near(step)[1], 6)

    @pl.when(has_after)
    def _():
        send(hid_ref, hid_buf.at[0], after, 4)

    @pl.when(has_before)
    def _():
        send(hid_ref, hid_buf.at[1], before, 11)

    finish(near_buf.at[pl.ds(0, 3)], 6)
    far_buf[high] = (near_buf[0] + near_buf[1]) + (near_buf[2] + near_buf[3])
    pl.semaphore_wait(ready_sem, 1)
    for device in (opposite, across, beside):
        send(far_buf.at[high], far_buf.at[high], device, 7)

    @pl.when(has_before)
    def _():
        finish(hid_buf.at[0], 4)

    @pl.when(jnp.logical_not(has_before))
    def _():
        hid_buf[0] = jnp.zeros((128, 256), BF16)

    @pl.when(has_after)
    def _():
        finish(hid_buf.at[1], 11)

    @pl.when(jnp.logical_not(has_after))
    def _():
        hid_buf[1] = jnp.zeros((128, 256), BF16)

    def hid_of(ref):
        def part(n):
            return ref[...].astype(F32).reshape(8, 16, 256)[:, n * 8 : n * 8 + 8, :]

        return part

    fill_windows(
        win_hid, links_ref, position, hid_of(hid_buf.at[0]), hid_of(hid_ref), hid_of(hid_buf.at[1])
    )
    second = convolve(win_hid, band_two)
    fine = second.reshape(8, 16, 256) + lifted_ref[1]
    for n in range(2):
        fine_ref[n * 64 : n * 64 + 64] = fine[:, n * 8 : n * 8 + 8, :].reshape(64, 256).astype(BF16)
    scale = 1.0 / math.sqrt(8 * 128 * 512)
    finish(far_buf.at[pl.ds(0, 3)], 7)
    total_ref[me] = ((far_buf[0] + far_buf[1]) + (far_buf[2] + far_buf[3])) * scale
    for device in farthest_first():
        send(total_ref.at[me], total_ref.at[me], device, 8)
    finish(total_ref.at[pl.ds(0, 31)], 8)

    sums_ref[...] = total_ref[...]

    sent(y_buf.at[pl.ds(0, 3)], 0)
    sent(cross_buf, 1)
    sent(high_buf, 10)
    sent(low_buf.at[pl.ds(0, 3)], 2)

    @pl.when(has_after)
    def _():
        sent(cot_buf.at[0], 3)
        sent(hid_buf.at[0], 4)

    @pl.when(has_before)
    def _():
        sent(cot_buf.at[1], 9)
        sent(hid_buf.at[1], 11)

    sent(first_buf.at[pl.ds(0, 31)], 5)
    sent(near_buf.at[pl.ds(0, 3)], 6)
    sent(far_buf.at[pl.ds(0, 3)], 7)
    sent(total_ref.at[pl.ds(0, 31)], 8)


def unpack_kernel(sums_ref, given_ref, fine_ref, grad_one_ref, grad_two_ref):
    fine_ref[...] = given_ref[...]
    for k in range(7):
        packed = sums_ref[2 * k : 2 * k + 2].reshape(32, 128)
        turned = jnp.transpose(packed).reshape(4, 32, 32)
        count = min(4, 27 - 4 * k)
        grad_one_ref[4 * k : 4 * k + count] = turned[0:count]
        packed = sums_ref[14 + 2 * k : 14 + 2 * k + 2].reshape(32, 128)
        for j in range(count):
            moved = packed if j == 0 else pltpu.roll(packed, 128 - 32 * j, 1)
            grad_two_ref[4 * k + j] = moved[:, 0:32]


def body(coarse_latents, active_blocks, face_links, cotangent, up_weight, conv_one, conv_two):
    vmem = pl.BlockSpec(memory_space=pltpu.VMEM)
    outside = pl.BlockSpec(memory_space=pl.ANY)
    scratch = [
        ((528, 128), BF16),
        ((4, 144, 128), BF16),
        ((144, 128), BF16),
        ((80, 128), BF16),
        ((80, 128), BF16),
        ((48, 128), BF16),
        ((48, 128), F32),
        ((4, 24, 128), F32),
        ((2, 128, 256), BF16),
        ((128, 256), BF16),
        ((2, 128, 256), BF16),
        ((864, 256), F32),
        ((864, 256), F32),
        ((3, 1024, 256), BF16),
        ((3, 1024, 256), BF16),
        ((3, 256, 1024), BF16),
        ((512, 1024), BF16),
        ((3, 8, 16, 256), F32),
        ((10, 16, 1024), BF16),
        ((10, 16, 1024), BF16),
        ((10, 16, 1024), BF16),
        ((32, 16, 128), F32),
        ((32, 16, 128), F32),
        ((4, 16, 128), F32),
        ((4, 16, 128), F32),
        ((32, 16, 128), F32),
    ]
    inputs = [
        pltpu.VMEM((64, 512), BF16),
        pltpu.VMEM((1, 128), jnp.int32),
        pltpu.SMEM((2, 6), jnp.int32),
        pltpu.VMEM((128, 256), BF16),
        pltpu.VMEM((64, 2048), BF16),
        pltpu.VMEM((864, 32), BF16),
        pltpu.VMEM((864, 32), BF16),
    ]
    out_shape = (
        jax.ShapeDtypeStruct((128, 256), BF16),
        jax.ShapeDtypeStruct((32, 16, 128), F32),
    )
    given, sums = pl.pallas_call(
        step_kernel,
        out_shape=out_shape,
        in_specs=[outside] * 7,
        out_specs=(vmem, vmem),
        scratch_shapes=inputs
        + [pltpu.VMEM(*one) for one in scratch]
        + [pltpu.SemaphoreType.DMA((count,)) for count in (13, 13, 7)]
        + [pltpu.SemaphoreType.REGULAR],
        compiler_params=pltpu.CompilerParams(
            collective_id=0, has_side_effects=True, vmem_limit_bytes=62 * 1024 * 1024
        ),
    )(
        coarse_latents[0],
        active_blocks,
        face_links[0],
        cotangent.reshape(128, 256),
        up_weight,
        conv_one.reshape(864, 32),
        conv_two.reshape(864, 32),
    )
    fine, grad_one, grad_two = pl.pallas_call(
        unpack_kernel,
        out_shape=(
            jax.ShapeDtypeStruct((128, 256), BF16),
            jax.ShapeDtypeStruct((27, 32, 32), F32),
            jax.ShapeDtypeStruct((27, 32, 32), F32),
        ),
        in_specs=[vmem] * 2,
        out_specs=(vmem,) * 3,
    )(sums, given)
    return fine.reshape(1, 2, 8, 8, 256), grad_one, grad_two


def solution(mesh):
    return jax.shard_map(
        body,
        mesh=mesh,
        in_specs=(
            P("dp", "space", None),
            P("dp", None),
            P("dp", "space", None),
            P("dp", "space", None, None, None),
            P(),
            P(),
            P(),
        ),
        out_specs=(P("dp", "space", None, None, None), P(), P()),
        check_vma=False,
    )
```
